32 devices in a mesh: lat: 4 (over y, core), lon: 8 (over z, x).
Axes of the slice: x: 2, y: 2, z: 4, core: 2. Of those that a mesh axis runs over, the one named last changes fastest.
Arguments:
- obs_pert: bfloat16 [1024, 512, 256], P(('lat', 'lon')), may hold values from -3 to 3
- obs_weight: bfloat16 [1024, 512], P(('lat', 'lon')), may hold values from 0.5 to 2
- innovation: bfloat16 [1024, 512], P(('lat', 'lon')), may hold values from -6 to 6
- batch_len: int32 [32, 32], P(('lat', 'lon')), may hold values from 1 to 512, 10240 in all within a row
- batch_owner: int32 [1024, 1], P(('lat', 'lon')), may hold values from 0 to 7; in each aligned block of 32 rows (0 to 31, 32 to 63, ...) at most 4 rows name the same one
- batch_points: int32 [1024, 3], P(('lat', 'lon')), may hold values from 0 to 7, all different within a row
- batch_count: int32 [1024], P(('lat', 'lon')), may hold values from 1 to 3
- batch_taper: bfloat16 [1024, 3], P(('lat', 'lon')), may hold values from 0.25 to 1
- background: bfloat16 [32, 1024, 256], P('lat', 'lon'), may hold values from -6 to 6
- stencil: int32 [2, 32, 1024], P(None, 'lat', 'lon'), may hold values from 0 to 31, as said below
- frac: float32 [2, 32, 1024], P(None, 'lat', 'lon'), may hold values from 0 to 1
Outputs:
- analysis: bfloat16 [32, 1024, 256], P('lat', 'lon')
The draws below stay inside these ranges and needn't reach their ends.
Inputs may be any that keep to these rules, and one draw needn't show every extreme that they name: `batch_owner`: among the 32 batches held by one device, at most 4 share an owner, and in every draw some owner has exactly 4 of them. `batch_points`: the entries of a row are distinct; local point p of an owner is its point p // 4 along latitude and p % 4 along longitude. Only the first batch_count entries of a batch's row of batch_points and batch_taper count. `batch_len`: each row sums to 10240 and its largest entry is 512. For a cell in the block of cells a * 8 .. (a + 1) * 8 - 1 along latitude and c * 128 .. (c + 1) * 128 - 1 along longitude, stencil[0] lies in a * 2 - 1 .. (a + 1) * 2 - 1 and in 0 .. 6, and stencil[1] is (c * 4 - 1 + t) mod 32 for some t in 0 .. 4.
All inputs are finite; a program needn't handle non-finite values.
Results may differ from the reference program's by a relative error of at most 0.0059.
Values may be sent and summed in bfloat16 or wider, within the bound.
No kernel may reach another device: no remote copies, remote signals or barrier semaphores. Data moves between devices by JAX's collectives and lax.ppermute only.
A program may use at most 128 MiB of HBM per device.

```python
import math
import jax
import jax.numpy as jnp
import numpy as np
from jax import lax

MEMBERS = 256
NOBS = 512
BAT_DEV = 32
CAP = 4
TOP = 3
PLAT = 2
PLON = 4
PTS_DEV = 8
CLAT = 8
CLON = 128
ITERS = 6
BATCHES = 1024
NPLAT = 8
NPLON = 32
NCLAT = 32
NCLON = 1024
N_LAT = 4
N_LON = 8


def draw_stencil(key, part):
    lat_key = jax.random.fold_in(key, 11)
    lon_key = jax.random.fold_in(key, 23)
    lat_block = jnp.arange(NCLAT, dtype=jnp.int32) // CLAT
    lon_block = jnp.arange(NCLON, dtype=jnp.int32) // CLON
    lat_step = jax.random.randint(lat_key, (NCLAT, NCLON), 0, PLAT + 1, dtype=jnp.int32)
    lon_step = jax.random.randint(lon_key, (NCLAT, NCLON), 0, PLON + 1, dtype=jnp.int32)
    lat_index = jnp.clip(lat_block[:, None] * PLAT - 1 + lat_step, 0, NPLAT - 2)
    lon_index = (lon_block[None, :] * PLON - 1 + lon_step) % NPLON
    return jnp.stack([lat_index, lon_index]).astype(jnp.int32)


def plant(drawn, rng, least, high):
    place = [jax.random.randint(jax.random.fold_in(rng, axis), (), 0, length) for axis, length in enumerate(drawn.shape)]
    widest = drawn.shape.index(max(drawn.shape))
    beside = place[:widest] + [(place[widest] + 1) % drawn.shape[widest]] + place[widest + 1:]
    return drawn.at[tuple(place)].set(least).at[tuple(beside)].set(high)


def shard_levels(rng, extent, cuts, least, top_value):
    def one(dim, shards_of):
        steps = jax.random.uniform(jax.random.fold_in(jax.random.fold_in(rng, 6), dim), (shards_of,), jnp.float32, least / len(cuts), top_value / len(cuts))
        return jnp.repeat(jnp.exp(steps), extent[dim] // shards_of).reshape((-1,) + (1,) * (len(extent) - dim - 1))

    loudness = one(*cuts[0])
    for cut in cuts[1:]:
        loudness = loudness * one(*cut)
    return loudness


def choose_distinct(stream_key, rows, count, top, lift):
    sequence = jax.random.permutation(jax.random.fold_in(stream_key, 1), count)
    pull = sequence
    for power in range(3):
        pull = pull * pull // count
    pull = pull * lift // count
    tickets = jax.random.randint(jax.random.fold_in(stream_key, 2), (rows, count), 0, 4096) + pull
    holders = jax.random.permutation(jax.random.fold_in(stream_key, 3), rows)[jnp.arange(count) % rows]
    tickets = jnp.where(jnp.arange(rows)[:, None] == holders[None, :], 1 << 14, tickets)
    priority = tickets * count + jnp.arange(count)
    return lax.top_k(priority.astype(jnp.int32), top)[1].astype(jnp.int32)


def split_up(number_of, total, bound, slope):
    portions = [(1 << 20) // math.isqrt(grade ** slope) + 1 for grade in range(2, number_of + 1)]
    surplus, holding = total - bound - (number_of - 1), [1] * (number_of - 1)
    while surplus > 0:
        candidates = [i for i in range(number_of - 1) if holding[i] < bound]
        mass, left = sum([portions[i] for i in candidates]), surplus
        for i in candidates:
            more = min(bound - holding[i], max(1, left * portions[i] // mass), surplus)
            holding[i] = holding[i] + more
            surplus = surplus - more
    return np.array([bound] + holding)


def ragged(stream_key, number_of, total, limit, skew):
    if number_of == 2:
        one = jax.random.randint(stream_key, (), max(1, total - limit), min(limit, total - 1) + 1)
        return jnp.stack([one, total - one])
    sizes = jnp.asarray(split_up(number_of, total, limit, skew), jnp.int32)
    couples = (number_of - 1) // 2
    giver, receiver = sizes[1:1 + 2 * couples:2], sizes[2:2 + 2 * couples:2]
    room = jnp.minimum(giver - 1, limit - receiver)
    moved = jax.random.randint(jax.random.fold_in(stream_key, 1), (couples,), 0, 1 << 20) % (room + 1)
    sizes = sizes.at[1:1 + 2 * couples:2].set(giver - moved).at[2:2 + 2 * couples:2].set(receiver + moved)
    return sizes[jax.random.permutation(jax.random.fold_in(stream_key, 2), number_of)]


def assign_block(own_key, own, number, rows, number_of, top, bound, lean):
    order = jax.random.permutation(own_key, number_of)
    crowded, ordinary = load_shares(number_of, rows * top, bound, lean, True), load_shares(number_of, rows * top, bound, lean, False)
    places = jnp.arange(number_of)

    def named(sizes, offset_by):
        used = int((sizes > 0).sum())
        fixed = max(1, used // 4)
        shifted = fixed + (places - fixed + offset_by * (used - fixed)) % max(1, number_of - fixed)
        return jnp.zeros((number_of,), jnp.int32).at[order[jnp.where(places < fixed, places, shifted)]].set(jnp.asarray(sizes, jnp.int32))

    sizes = jnp.where(number % 4 == 0, named(crowded, number // 4), named(ordinary, number - number // 4 - 1))
    mixed = jax.random.permutation(jax.random.fold_in(own, 3), number_of)
    giver, receiver = mixed[0:number_of // 2 * 2:2], mixed[1:number_of // 2 * 2:2]
    room = jnp.minimum(sizes[giver] - 1, bound - sizes[receiver]) // 2
    room = jnp.where((giver == order[0]) | (receiver == order[0]) | (sizes[receiver] == 0), 0, jnp.maximum(room, 0))
    shifted = jax.random.randint(jax.random.fold_in(own, 4), (number_of // 2,), 0, 1 << 20) % (room + 1)
    sizes = sizes.at[giver].add(-shifted).at[receiver].add(shifted)
    items = jnp.searchsorted(jnp.cumsum(sizes), jnp.arange(rows * top), side="right").astype(jnp.int32)
    table = items.reshape(top, rows).T
    table = table[jax.random.permutation(jax.random.fold_in(own, 1), rows)]
    offset_by = jax.random.randint(jax.random.fold_in(own, 2), (rows, 1), 0, top)
    return jnp.take_along_axis(table, (jnp.arange(top)[None, :] + offset_by) % top, axis=1)


def load_shares(count, total, reach, slope, full):
    portions = [(1 << 20) // math.isqrt(grade ** slope) + 1 for grade in range(1, count + 1)]
    largest = reach if full else min(reach, max(-(-total // count), total * portions[0] // sum(portions)))
    least = 1 if total - largest >= count - 1 else 0
    given, rest = [largest] + [least] * (count - 1), total - largest - least * (count - 1)
    while rest > 0:
        free = [i for i in range(1, count) if given[i] < largest] or [i for i in range(1, count) if given[i] < reach]
        pool, remaining = sum([portions[i] for i in free]), rest
        for i in free:
            addition = min(reach - given[i], max(1, remaining * portions[i] // pool), rest)
            given[i] = given[i] + addition
            rest = rest - addition
    return np.array(given)


def bell_draw(own_key, shape, scale, bound, cuts=(), kind=jnp.bfloat16):
    values = scale * jax.random.normal(own_key, shape, jnp.float32)
    if cuts:
        values = values * shard_levels(own_key, shape, cuts, -0.22, 0.18)
    return jnp.clip(values, -bound, bound).astype(kind)


def setup_inputs(seed: int = 0) -> dict:
    key_list = jax.random.split(jax.random.key(seed), 12)
    obs_pert = bell_draw(key_list[0], (BATCHES, NOBS, MEMBERS), 0.5, 3.0, ((0, 32),))
    obs_weight = jnp.clip(jnp.exp(math.log(2.0) - 1.3862944 * jax.random.uniform(key_list[1], (BATCHES, NOBS), jnp.float32) ** shard_levels(key_list[1], (BATCHES, NOBS), ((0, 32),), -0.2, 0.2)), 0.5, 2.0).astype(jnp.bfloat16)
    innovation = bell_draw(key_list[2], (BATCHES, NOBS), 1.0, 6.0, ((0, 32),))
    batch_len = jax.vmap(lambda own: ragged(own, BAT_DEV, BAT_DEV * NOBS * 5 // 8, NOBS, 2))(jax.random.split(key_list[3], (N_LAT * N_LON))).reshape((N_LAT * N_LON, BAT_DEV)).astype(jnp.int32)
    batch_owner_keys = jax.random.split(jax.random.fold_in(key_list[4], 1), BATCHES // BAT_DEV)
    batch_owner_turns = jax.random.permutation(jax.random.fold_in(key_list[4], 3), BATCHES // BAT_DEV)
    batch_owner = jax.vmap(lambda own, number: assign_block(jax.random.fold_in(key_list[4], 2), own, number, BAT_DEV, N_LON, 1, CAP, 2))(batch_owner_keys, batch_owner_turns).reshape((BATCHES, 1))
    batch_points = choose_distinct(key_list[5], BATCHES, PTS_DEV, TOP, 0)
    batch_count = plant(jax.random.randint(key_list[6], (BATCHES,), 1, TOP + 1), jax.random.fold_in(key_list[6], 1), 1, TOP).astype(jnp.int32)
    batch_taper = jnp.clip(jnp.exp(math.log(1.0) - 1.3862944 * jax.random.uniform(key_list[7], (BATCHES, TOP), jnp.float32) ** shard_levels(key_list[7], (BATCHES, TOP), ((0, 32),), -0.2, 0.2)), 0.25, 1.0).astype(jnp.bfloat16)
    background = bell_draw(key_list[8], (NCLAT, NCLON, MEMBERS), 1.0, 6.0, ((0, 4), (1, 8)))
    stencil = draw_stencil(jax.random.fold_in(key_list[11], 71), 0)
    frac = jnp.clip(1.0 * jax.random.uniform(key_list[10], (2, NCLAT, NCLON), jnp.float32) ** shard_levels(key_list[10], (2, NCLAT, NCLON), ((1, 4), (2, 8)), -0.2, 0.2), 0.0, 1.0)
    return dict(obs_pert=obs_pert, obs_weight=obs_weight, innovation=innovation, batch_len=batch_len, batch_owner=batch_owner, batch_points=batch_points, batch_count=batch_count, batch_taper=batch_taper, background=background, stencil=stencil, frac=frac)


def one_batch(item):
    pert_rows, weight_rows, innov_rows, length = item
    live_rows = (jnp.arange(NOBS) < length).astype(jnp.float32)
    kept = weight_rows.astype(jnp.float32) * live_rows
    scaled = (kept[:, None] * pert_rows.astype(jnp.float32)).astype(jnp.bfloat16)
    batch_gram = jnp.dot(scaled.T, pert_rows, preferred_element_type=jnp.float32).astype(jnp.bfloat16)
    batch_proj = jnp.dot(innov_rows, scaled, preferred_element_type=jnp.float32).astype(jnp.bfloat16)
    return (batch_gram, batch_proj)

def point_weights(batch_points, batch_count, batch_taper):
    listed = jnp.arange(TOP, dtype=jnp.int32)
    valid = listed[None, :] < batch_count[:, None]
    onehot = batch_points[:, :, None] == jnp.arange(PTS_DEV, dtype=jnp.int32)[None, None, :]
    picked = jnp.where(valid[:, :, None] & onehot, batch_taper.astype(jnp.float32)[:, :, None], jnp.float32(0.0))
    return lax.optimization_barrier(jnp.sum(picked, axis=1)).astype(jnp.bfloat16)

def analysis_transform(item):
    total, shift = item
    identity = jnp.eye(MEMBERS, dtype=jnp.float32)
    system = total + (MEMBERS - 1) * identity
    scale = jnp.sqrt(jnp.sum(system * system))
    iterate = system / scale
    inverse_root = identity
    for sweep in range(ITERS):
        factor = 1.5 * identity - 0.5 * jnp.dot(inverse_root, iterate, precision=lax.Precision.HIGHEST)
        iterate = jnp.dot(iterate, factor, precision=lax.Precision.HIGHEST)
        inverse_root = jnp.dot(factor, inverse_root, precision=lax.Precision.HIGHEST)
    inner = jnp.dot(inverse_root, shift, precision=lax.Precision.HIGHEST)
    mean_weight = jnp.dot(inverse_root, inner, precision=lax.Precision.HIGHEST) / scale
    result = jnp.sqrt((MEMBERS - 1) / scale) * inverse_root + mean_weight[:, None]
    return result.astype(jnp.bfloat16)

def interp_weights(stencil, frac, lat_pos, lon_pos, point_cols):
    row_off = stencil[0] - (lat_pos * PLAT - 1)
    col_off = (stencil[1] - lon_pos * PLON + 1) % point_cols
    lat_frac = frac[0].reshape(-1)[:, None]
    lon_frac = frac[1].reshape(-1)[:, None]
    corner_id = (row_off * (PLON + 2) + col_off).reshape(-1)[:, None]
    all_ids = jnp.arange((PLAT + 2) * (PLON + 2), dtype=jnp.int32)[None, :]
    zero_val = jnp.float32(0.0)
    weights = jnp.where(corner_id == all_ids, (1.0 - lat_frac) * (1.0 - lon_frac), zero_val)
    weights = weights + jnp.where(corner_id + (PLON + 2) == all_ids, lat_frac * (1.0 - lon_frac), zero_val)
    weights = weights + jnp.where(corner_id + 1 == all_ids, (1.0 - lat_frac) * lon_frac, zero_val)
    weights = weights + jnp.where(corner_id + (PLON + 3) == all_ids, lat_frac * lon_frac, zero_val)
    return weights

def reference(obs_pert, obs_weight, innovation, batch_len, batch_owner, batch_points, batch_count, batch_taper, background, stencil, frac):
    lengths = batch_len.reshape(-1)
    grams, projs = lax.map(one_batch, (obs_pert, obs_weight, innovation, lengths))
    coef = point_weights(batch_points, batch_count, batch_taper)
    band_size = N_LON * BAT_DEV
    owners = batch_owner[:, 0].reshape(N_LAT, band_size)
    coef_rows = coef.reshape(N_LAT, band_size, PTS_DEV)
    gram_rows = grams.reshape(N_LAT, band_size, MEMBERS * MEMBERS)
    proj_rows = projs.reshape(N_LAT, band_size, MEMBERS)

    def one_band(item):
        band_owner, band_coef, band_gram, band_proj = item
        local = jnp.arange(PTS_DEV, dtype=jnp.int32)
        target = (local // PLON)[None, :] * NPLON + band_owner[:, None] * PLON + (local % PLON)[None, :]
        hit_table = target[None, :, :] == jnp.arange(PLAT * NPLON, dtype=jnp.int32)[:, None, None]
        mixing = lax.optimization_barrier(jnp.sum(jnp.where(hit_table, band_coef.astype(jnp.float32)[None], jnp.float32(0.0)), axis=2))
        totals = jnp.dot(mixing, band_gram.astype(jnp.float32), precision=lax.Precision.HIGHEST)
        shifts = jnp.dot(mixing, band_proj.astype(jnp.float32), precision=lax.Precision.HIGHEST)
        return (totals, shifts)
    totals, shifts = lax.map(one_band, (owners, coef_rows, gram_rows, proj_rows))
    transforms = lax.map(analysis_transform, (totals.reshape(-1, MEMBERS, MEMBERS), shifts.reshape(-1, MEMBERS)))
    transforms = transforms.reshape(NPLAT, NPLON, MEMBERS, MEMBERS)
    mean_field = lax.optimization_barrier(jnp.mean(background.astype(jnp.float32), axis=-1))
    deviation = (background.astype(jnp.float32) - mean_field[..., None]).astype(jnp.bfloat16)
    zero_idx = jnp.zeros((), jnp.int32)

    def one_tile(tile):
        lat_pos = (tile // N_LON).astype(jnp.int32)
        lon_pos = (tile % N_LON).astype(jnp.int32)
        rows = (lat_pos * PLAT - 1 + jnp.arange(PLAT + 2, dtype=jnp.int32)) % NPLAT
        cols = (lon_pos * PLON - 1 + jnp.arange(PLON + 2, dtype=jnp.int32)) % NPLON
        window = transforms[rows][:, cols].reshape(-1, MEMBERS, MEMBERS)
        cells = lax.dynamic_slice(deviation, (lat_pos * CLAT, lon_pos * CLON, zero_idx), (CLAT, CLON, MEMBERS))
        tile_mean = lax.dynamic_slice(mean_field, (lat_pos * CLAT, lon_pos * CLON), (CLAT, CLON))
        tile_sten = lax.dynamic_slice(stencil, (zero_idx, lat_pos * CLAT, lon_pos * CLON), (2, CLAT, CLON))
        tile_frac = lax.dynamic_slice(frac, (zero_idx, lat_pos * CLAT, lon_pos * CLON), (2, CLAT, CLON))
        weights = interp_weights(tile_sten, tile_frac, lat_pos, lon_pos, NPLON)
        products = jnp.einsum('ck,jkl->cjl', cells.reshape(-1, MEMBERS).astype(jnp.float32), window.astype(jnp.float32), precision=lax.Precision.HIGHEST)
        mixed = jnp.einsum('cj,cjl->cl', weights, products, precision=lax.Precision.HIGHEST)
        return (tile_mean.reshape(-1)[:, None] + mixed).astype(jnp.bfloat16)
    tiles = lax.map(one_tile, jnp.arange(N_LAT * N_LON, dtype=jnp.int32))
    tiles = tiles.reshape(N_LAT, N_LON, CLAT, CLON, MEMBERS)
    return jnp.transpose(tiles, (0, 2, 1, 3, 4)).reshape(NCLAT, NCLON, MEMBERS)
```

```python
import functools

import jax
import jax.numpy as jnp
from jax import lax
from jax.experimental import pallas as pl
from jax.experimental.pallas import tpu as pltpu
from jax.sharding import PartitionSpec as P

CAP = 4
PLAT = 2
PLON = 4
POINTS = PLAT * PLON
ITERS = 6
HALF = 128
MEMBERS = 2 * HALF
TILE = 16
BLOCK = CAP * MEMBERS + TILE
PACKED = MEMBERS + TILE
F32 = jnp.float32
BF16 = jnp.bfloat16
VMEM_LIMIT = 56 * 1024 * 1024

SMEM_SPEC = pl.BlockSpec(memory_space=pltpu.SMEM)
VMEM_SPEC = pl.BlockSpec(memory_space=pltpu.VMEM)
ANY_SPEC = pl.BlockSpec(memory_space=pl.ANY)


def params():
    return pltpu.CompilerParams(vmem_limit_bytes=VMEM_LIMIT)


def dot_nn(a, b):
    return lax.dot_general(a, b, (((1,), (0,)), ((), ())), preferred_element_type=F32)


def dot_nt(a, b):
    return lax.dot_general(a, b, (((1,), (1,)), ((), ())), preferred_element_type=F32)


def iota(shape, dim):
    return lax.broadcasted_iota(jnp.int32, shape, dim)


def partner_of(me, offset, lon_size):
    if lon_size & (lon_size - 1) == 0:
        return me ^ offset
    return lax.rem(me + offset, lon_size)


def partner_pairs(offset, lon_size):
    if lon_size & (lon_size - 1) == 0:
        return [(i, i ^ offset) for i in range(lon_size)]
    return [(i, (i + offset) % lon_size) for i in range(lon_size)]


def gram_kernel(first, count, lon_size, me_ref, owner_ref, len_ref, points_ref, num_ref,
                weight_ref, innov_ref, taper_ref, pert_ref, *rest):
    outs, (source, filled, rows, w32, i32, t32, built, in_sem, out_sem) = rest[:count], rest[count:]
    held = pert_ref.shape[0]
    me = me_ref[0]
    nobs = pert_ref.shape[1]

    @pl.loop(0, lon_size * CAP)
    def _(s):
        source[s] = -1

    @pl.loop(0, lon_size)
    def _(k):
        filled[k] = 0

    @pl.loop(0, held)
    def _(b):
        owner = owner_ref[b, 0]
        if lon_size & (lon_size - 1) == 0:
            k = owner ^ me
        else:
            k = lax.rem(owner - me + lon_size, lon_size)
        n = filled[k]
        source[k * CAP + n] = b
        filled[k] = n + 1

    def fetch(k, j):
        b = jnp.maximum(source[k * CAP + j], 0)
        return pltpu.make_async_copy(pert_ref.at[b], rows.at[j], in_sem.at[j])

    for j in range(CAP):
        fetch(first, j).start()
    w32[...] = weight_ref[...].astype(F32)
    i32[...] = innov_ref[...].astype(F32)
    t32[:, 0:3] = taper_ref[...].astype(F32)
    lane_obs = iota((1, nobs), 1)
    lane = iota((1, HALF), 1)
    row_id = iota((HALF, HALF), 0)
    col_id = iota((HALF, HALF), 1)

    @pl.loop(0, count)
    def _(step):
        k = first + step
        lo, hi, dg, cf = [], [], [], []
        for j in range(CAP):
            b = source[k * CAP + j]
            present = b >= 0
            b = jnp.maximum(b, 0)
            fetch(k, j).wait()
            live = jnp.where(present, len_ref[0, b], 0)
            keep = jnp.where(lane_obs < live, w32[pl.ds(b, 1), :], 0.0)
            pulled = (keep * i32[pl.ds(b, 1), :]).astype(BF16)
            x = rows[j]
            xt = x.T
            scaled = xt * keep.astype(BF16)
            lhs = jnp.concatenate([scaled, jnp.broadcast_to(pulled, (TILE, nobs))], axis=0)
            gram = dot_nn(lhs, x)
            a11 = gram[0:HALF, 0:HALF]
            a22 = gram[HALF:MEMBERS, HALF:MEMBERS]
            built[step, pl.ds(j * MEMBERS, HALF), :] = jnp.where(row_id <= col_id, a11, a22).astype(BF16)
            built[step, pl.ds(j * MEMBERS + HALF, HALF), :] = gram[0:HALF, HALF:MEMBERS].astype(BF16)
            lo.append(gram[MEMBERS:MEMBERS + 1, 0:HALF])
            hi.append(gram[MEMBERS:MEMBERS + 1, HALF:MEMBERS])
            dg.append(jnp.sum(jnp.where(row_id == col_id, a22, 0.0), axis=0, keepdims=True))
            taper = t32[pl.ds(b, 1), :]
            limit = jnp.where(present, num_ref[b], 0)
            coef = jnp.zeros((1, HALF), F32)
            for q in range(3):
                hit = (lane == points_ref[b, q]) & (q < limit)
                coef = coef + jnp.where(hit, taper[:, q:q + 1], 0.0)
            cf.append(coef)

            @pl.when(step + 1 < count)
            def _():
                fetch(k + 1, j).start()

        built[step, pl.ds(CAP * MEMBERS, TILE), :] = jnp.concatenate(lo + hi + dg + cf, axis=0).astype(BF16)
        for i in range(count):
            @pl.when(step == i)
            def _():
                pltpu.make_async_copy(built.at[i], outs[i], out_sem.at[i]).start()

    for i in range(count):
        pltpu.make_async_copy(built.at[i], outs[i], out_sem.at[i]).wait()


def batch_blocks(first, count, lon_size, me, owner, length, points, num, weight, innov, taper, pert):
    held, nobs, members = pert.shape
    return pl.pallas_call(
        functools.partial(gram_kernel, first, count, lon_size),
        out_shape=[jax.ShapeDtypeStruct((BLOCK, HALF), BF16)] * count,
        in_specs=[SMEM_SPEC] * 5 + [VMEM_SPEC] * 3 + [ANY_SPEC],
        out_specs=[ANY_SPEC] * count,
        scratch_shapes=[
            pltpu.SMEM((lon_size * CAP,), jnp.int32),
            pltpu.SMEM((lon_size,), jnp.int32),
            pltpu.VMEM((CAP, nobs, members), BF16),
            pltpu.VMEM((held, nobs), F32),
            pltpu.VMEM((held, nobs), F32),
            pltpu.VMEM((held, HALF), F32),
            pltpu.VMEM((count, BLOCK, HALF), BF16),
            pltpu.SemaphoreType.DMA((CAP,)),
            pltpu.SemaphoreType.DMA((count,)),
        ],
        compiler_params=params(),
        cost_estimate=pl.CostEstimate(
            flops=count * CAP * 2 * nobs * members * members,
            bytes_accessed=count * CAP * nobs * members * 2, transcendentals=0),
    )(me, owner, length, points, num, weight, innov, taper, pert)


def unpack(triangle, corner, diagonal):
    row_id = iota((HALF, HALF), 0)
    col_id = iota((HALF, HALF), 1)
    flipped = triangle.T
    a11 = jnp.where(row_id <= col_id, triangle, flipped)
    a22 = jnp.where(row_id > col_id, triangle, jnp.where(row_id == col_id, diagonal, flipped))
    return jnp.concatenate(
        [jnp.concatenate([a11, corner], axis=1), jnp.concatenate([corner.T, a22], axis=1)], axis=0)


def mm(a, b):
    return dot_nn(a.astype(BF16), b.astype(BF16))


def transform_points(listed, total_of, side_of, wz, out_of):
    eye = (iota((MEMBERS, MEMBERS), 0) == iota((MEMBERS, MEMBERS), 1)).astype(F32)
    scales = []
    for i, p in enumerate(listed):
        packed = total_of(p)
        system = unpack(packed[0:HALF], packed[HALF:MEMBERS], side_of(p)[2]) + (MEMBERS - 1) * eye
        square = jnp.sum(jnp.sum(system * system, axis=0, keepdims=True), axis=1, keepdims=True)
        inv = lax.rsqrt(square)
        inv = inv * (1.5 - 0.5 * square * inv * inv)
        scales.append(inv)
        wz[0, i] = system * inv
        wz[1, i] = 1.5 * eye - 0.5 * wz[0, i]
    count = len(listed)

    def advance(i):
        w = wz[0, i]
        wb = w.astype(BF16)
        u = dot_nn(wb, wb)
        wz[0, i] = 2.25 * w - 1.5 * u + 0.25 * dot_nn(wb, u.astype(BF16))

    def apply(i):
        z = wz[1, i]
        wz[1, i] = 1.5 * z - 0.5 * mm(wz[0, i], z)

    for i in range(count):
        advance(i)

    @pl.loop(0, ITERS - 2)
    def _(sweep):
        for i in range(count):
            apply(i)
            advance(i)

    for i in range(count):
        apply(i)
    row_id = iota((HALF, HALF), 0)
    col_id = iota((HALF, HALF), 1)
    for i, p in enumerate(listed):
        root = wz[1, i]
        low, high, _ = side_of(p)
        shift = jnp.concatenate([low, high], axis=1)
        inner = jnp.sum(root * shift, axis=1, keepdims=True)
        mean_weight = jnp.sum(root * inner, axis=0, keepdims=True) * scales[i]
        result = root * jnp.sqrt((MEMBERS - 1) * scales[i])
        a22 = result[HALF:MEMBERS, HALF:MEMBERS]
        ref, where = out_of(p)
        ref[where, pl.ds(0, HALF), :] = jnp.where(row_id <= col_id, result[0:HALF, 0:HALF], a22).astype(BF16)
        ref[where, pl.ds(HALF, HALF), :] = result[0:HALF, HALF:MEMBERS].astype(BF16)
        diagonal = jnp.sum(jnp.where(row_id == col_id, a22, 0.0), axis=0, keepdims=True)
        extra = jnp.concatenate(
            [diagonal, mean_weight[:, 0:HALF], mean_weight[:, HALF:MEMBERS], jnp.zeros((TILE - 3, HALF), F32)],
            axis=0)
        ref[where, pl.ds(MEMBERS, TILE), :] = extra.astype(BF16)


def edge_kernel(lon_size, *refs):
    blocks = refs[:lon_size]
    left_ref, right_ref, total_ref, side_ref, wz, acc = refs[lon_size:]
    slots = lon_size * CAP
    extras = [blk[pl.ds(CAP * MEMBERS, TILE), :].astype(F32) for blk in blocks]
    low, high, diag, coef = [
        jnp.concatenate([e[CAP * q:CAP * (q + 1)] for e in extras], axis=0).astype(BF16) for q in range(4)]
    pick = (iota((POINTS, HALF), 0) == iota((POINTS, HALF), 1)).astype(BF16)
    by_point = dot_nt(pick, coef).astype(BF16)
    for q, part in enumerate((low, high, diag)):
        side_ref[q] = dot_nn(by_point, part)
    spread = (iota((POINTS * TILE, HALF), 0) // TILE == iota((POINTS * TILE, HALF), 1)).astype(BF16)
    tall = dot_nt(spread, coef).astype(BF16)
    wide = (iota((slots, slots * TILE), 1) // TILE == iota((slots, slots * TILE), 0)).astype(BF16)
    mixing = dot_nn(tall, wide)
    shape = (POINTS * TILE, slots * TILE)
    mixing = jnp.where(iota(shape, 0) % TILE == iota(shape, 1) % TILE, mixing, 0.0).astype(BF16)
    for g in range(0, MEMBERS // TILE, 2):
        pair = []
        for h in (g, g + 1):
            pair.append(jnp.concatenate(
                [blk[pl.ds(j * MEMBERS + h * TILE, TILE), :] for blk in blocks for j in range(CAP)], axis=0))
        summed = dot_nn(mixing, jnp.concatenate(pair, axis=1))
        for p in range(POINTS):
            for h in (0, 1):
                acc[p, pl.ds((g + h) * TILE, TILE), :] = summed[p * TILE:(p + 1) * TILE, h * HALF:(h + 1) * HALF]
    edge = [r * PLON + c for r in range(PLAT) for c in (0, PLON - 1)]
    inner = [p for p in range(POINTS) if p not in edge]
    for i, p in enumerate(inner):
        total_ref[i] = acc[p]
    transform_points(
        edge,
        lambda p: acc[p],
        lambda p: [side_ref[q, pl.ds(p, 1), :] for q in range(3)],
        wz,
        lambda p: (left_ref if p % PLON == 0 else right_ref, p // PLON))


def inner_kernel(total_in, side_in, out_ref, wz):
    edge = [r * PLON + c for r in range(PLAT) for c in (0, PLON - 1)]
    inner = [p for p in range(POINTS) if p not in edge]
    transform_points(
        inner,
        lambda p: total_in[inner.index(p)],
        lambda p: [side_in[q, pl.ds(p, 1), :] for q in range(3)],
        wz,
        lambda p: (out_ref, inner.index(p)))


def edge_transforms(blocks):
    lon_size = len(blocks)
    columns = jax.ShapeDtypeStruct((PLAT, PACKED, HALF), BF16)
    return pl.pallas_call(
        functools.partial(edge_kernel, lon_size),
        out_shape=[
            columns, columns,
            jax.ShapeDtypeStruct((POINTS - 2 * PLAT, MEMBERS, HALF), F32),
            jax.ShapeDtypeStruct((3, POINTS, HALF), F32),
        ],
        in_specs=[VMEM_SPEC] * lon_size,
        out_specs=[VMEM_SPEC] * 4,
        scratch_shapes=[
            pltpu.VMEM((2, 2 * PLAT, MEMBERS, MEMBERS), F32),
            pltpu.VMEM((POINTS, MEMBERS, HALF), F32),
        ],
        compiler_params=params(),
    )(*blocks)


def inner_transforms(total, side):
    count = total.shape[0]
    return pl.pallas_call(
        inner_kernel,
        out_shape=jax.ShapeDtypeStruct((count, PACKED, HALF), BF16),
        in_specs=[VMEM_SPEC] * 2,
        out_specs=VMEM_SPEC,
        scratch_shapes=[pltpu.VMEM((2, count, MEMBERS, MEMBERS), F32)],
        compiler_params=params(),
        cost_estimate=pl.CostEstimate(
            flops=count * 15 * 2 * MEMBERS ** 3, bytes_accessed=count * MEMBERS * HALF * 6, transcendentals=0),
    )(total, side)


def cell_kernel(point_cols, pos_ref, stencil_ref, frac_ref, field_ref, dev_ref, weight_ref):
    rows, width = stencil_ref.shape[1:]
    lat_pos, lon_pos = pos_ref[0], pos_ref[1]
    wide = PLON + 2
    ids = iota((HALF, width), 0)

    @pl.loop(0, rows)
    def _(i):
        x = field_ref[i].astype(F32)
        mean = jnp.mean(x, axis=1, keepdims=True)
        dev_ref[i] = (x - mean).astype(BF16)
        row_off = stencil_ref[0, pl.ds(i, 1), :] - (lat_pos * PLAT - 1)
        col_off = stencil_ref[1, pl.ds(i, 1), :] - (lon_pos * PLON - 1)
        col_off = jnp.where(col_off < 0, col_off + point_cols, col_off)
        col_off = jnp.where(col_off >= point_cols, col_off - point_cols, col_off)
        y = frac_ref[0, pl.ds(i, 1), :]
        x_frac = frac_ref[1, pl.ds(i, 1), :]
        corner = row_off * wide + col_off
        weights = jnp.where(corner == ids, (1.0 - y) * (1.0 - x_frac), 0.0)
        weights = weights + jnp.where(corner + wide == ids, y * (1.0 - x_frac), 0.0)
        weights = weights + jnp.where(corner + 1 == ids, (1.0 - y) * x_frac, 0.0)
        weights = weights + jnp.where(corner + wide + 1 == ids, y * x_frac, 0.0)
        turned = weights.T
        weight_ref[i] = jnp.where(iota((width, HALF), 1) == HALF - 1, mean, turned)


def cell_parts(point_cols, pos, stencil, frac, background):
    rows, width, members = background.shape
    return pl.pallas_call(
        functools.partial(cell_kernel, point_cols),
        out_shape=[
            jax.ShapeDtypeStruct((rows, width, members), BF16),
            jax.ShapeDtypeStruct((rows, width, HALF), F32),
        ],
        in_specs=[SMEM_SPEC] + [VMEM_SPEC] * 3,
        out_specs=[VMEM_SPEC] * 2,
        compiler_params=params(),
        cost_estimate=pl.CostEstimate(
            flops=rows * width * members * 4, bytes_accessed=rows * width * members * 6, transcendentals=0),
    )(pos, stencil, frac, background)


def mix_kernel(groups, final, tile_rows, *refs):
    n = len(groups)
    packed_refs = refs[:n]
    dev_ref, weight_ref = refs[n:n + 2]
    rest = refs[n + 2:]
    if final:
        base_ref, out_ref, matrices, lhs = rest
    else:
        out_ref, matrices, lhs = rest
    ids, extra_low, extra_high = [], [], []
    for ref, group in zip(packed_refs, groups):
        for i, point in enumerate(group):
            extra = ref[i, pl.ds(MEMBERS, TILE), :].astype(F32)
            full = unpack(
                ref[i, pl.ds(0, HALF), :].astype(F32), ref[i, pl.ds(HALF, HALF), :].astype(F32), extra[0:1])
            matrices[pl.ds(len(ids) * MEMBERS, MEMBERS), :] = full.astype(BF16)
            extra_low.append(extra[1:2])
            extra_high.append(extra[2:3])
            ids.append(point)
    count = len(ids)
    pad = jnp.zeros((HALF - count, HALF), F32)
    shifts = jnp.concatenate(
        [jnp.concatenate(extra_low + [pad], axis=0), jnp.concatenate(extra_high + [pad], axis=0)],
        axis=1).astype(BF16)
    rows, width, members = dev_ref.shape

    @pl.loop(0, rows // tile_rows)
    def _(t):
        dev_all = dev_ref[pl.ds(t * tile_rows, tile_rows)].reshape(tile_rows * width, members)
        weights = weight_ref[pl.ds(t * tile_rows, tile_rows)].reshape(tile_rows * width, HALF)
        spread = dev_all.astype(F32)
        shifted = dot_nt(dev_all, shifts)
        moved = jnp.zeros((tile_rows * width, 1), F32)
        for i, point in enumerate(ids):
            column = weights[:, point:point + 1]
            lhs[:, i * MEMBERS:(i + 1) * MEMBERS] = (spread * column).astype(BF16)
            moved = moved + column * shifted[:, i:i + 1]
        value = dot_nn(lhs[...], matrices[...]) + moved
        if final:
            value = value + weights[:, HALF - 1:HALF]
            value = value.reshape(tile_rows, width, members) + base_ref[pl.ds(t * tile_rows, tile_rows)]
            out_ref[pl.ds(t * tile_rows, tile_rows)] = value.astype(out_ref.dtype)
        else:
            out_ref[pl.ds(t * tile_rows, tile_rows)] = value.reshape(tile_rows, width, members)


def mix(groups, packed, dev, weights, base=None):
    rows, width, members = dev.shape
    count = sum(len(g) for g in groups)
    final = base is not None
    tile_rows = 2
    args = list(packed) + [dev, weights] + ([base] if final else [])
    return pl.pallas_call(
        functools.partial(mix_kernel, groups, final, tile_rows),
        out_shape=jax.ShapeDtypeStruct(dev.shape, BF16 if final else F32),
        in_specs=[VMEM_SPEC] * len(args),
        out_specs=VMEM_SPEC,
        scratch_shapes=[
            pltpu.VMEM((count * MEMBERS, MEMBERS), BF16),
            pltpu.VMEM((tile_rows * width, count * MEMBERS), BF16),
        ],
        compiler_params=params(),
        cost_estimate=pl.CostEstimate(
            flops=2 * rows * width * members * members * count,
            bytes_accessed=rows * width * members * 8, transcendentals=0),
    )(*args)


def on_device(obs_pert, obs_weight, innovation, batch_len, batch_owner, batch_points, batch_count,
              batch_taper, background, stencil, frac):
    lon_size, lat_size = lax.axis_size("lon"), lax.axis_size("lat")
    lat_pos, lon_pos = lax.axis_index("lat"), lax.axis_index("lon")
    me = lon_pos.astype(jnp.int32).reshape(1)
    pos = jnp.stack([lat_pos, lon_pos]).astype(jnp.int32)
    fixed = (me, batch_owner, batch_len, batch_points, batch_count, obs_weight, innovation, batch_taper, obs_pert)
    half = max(lon_size // 2, 1)
    far = batch_blocks(half, lon_size - half, lon_size, *fixed)
    got = [lax.ppermute(b, "lon", partner_pairs(half + i, lon_size)) for i, b in enumerate(far)]
    near = batch_blocks(0, half, lon_size, *fixed)
    got += [near[0]] + [lax.ppermute(b, "lon", partner_pairs(i, lon_size)) for i, b in enumerate(near) if i]
    dev, weights = cell_parts(PLON * lon_size, pos, stencil, frac, background)

    left, right, total, side = edge_transforms(got)
    up = [(i, (i + 1) % lon_size) for i in range(lon_size)]
    down = [(j, i) for i, j in up]
    before = lax.ppermute(right, "lon", up)
    after = lax.ppermute(left, "lon", down)
    inner = inner_transforms(total, side)
    inner_cols = PLON - 2

    def row_of(r):
        return jnp.concatenate(
            [before[r:r + 1], left[r:r + 1], inner[r * inner_cols:(r + 1) * inner_cols], right[r:r + 1],
             after[r:r + 1]], axis=0)

    north = [(i, i + 1) for i in range(lat_size - 1)]
    south = [(j, i) for i, j in north]
    below = lax.ppermute(row_of(PLAT - 1), "lat", north)
    above = lax.ppermute(row_of(0), "lat", south)
    wide = PLON + 2

    def ident(r, c):
        return (r + 1) * wide + c + 1

    own = [
        [ident(r, -1) for r in range(PLAT)],
        [ident(r, 0) for r in range(PLAT)],
        [ident(r, c) for r in range(PLAT) for c in range(1, PLON - 1)],
        [ident(r, PLON - 1) for r in range(PLAT)],
        [ident(r, PLON) for r in range(PLAT)],
    ]
    partial = mix(own, [before, left, inner, right, after], dev, weights)
    rims = [[ident(-1, c) for c in range(-1, PLON + 1)], [ident(PLAT, c) for c in range(-1, PLON + 1)]]
    return mix(rims, [below, above], dev, weights, partial)


def solution(mesh):
    return jax.shard_map(
        on_device,
        mesh=mesh,
        in_specs=(
            P(("lat", "lon"), None, None),
            P(("lat", "lon"), None),
            P(("lat", "lon"), None),
            P(("lat", "lon"), None),
            P(("lat", "lon"), None),
            P(("lat", "lon"), None),
            P(("lat", "lon")),
            P(("lat", "lon"), None),
            P("lat", "lon", None),
            P(None, "lat", "lon"),
            P(None, "lat", "lon"),
        ),
        out_specs=P("lat", "lon", None),
        check_vma=False,
    )
```

```python
import functools

import jax
import jax.numpy as jnp
from jax import lax
from jax.experimental import pallas as pl
from jax.experimental.pallas import tpu as pltpu
from jax.sharding import PartitionSpec as P

CAP = 4
PLAT = 2
PLON = 4
POINTS = PLAT * PLON
ITERS = 6
HALF = 128
MEMBERS = 2 * HALF
TILE = 16
BLOCK = CAP * MEMBERS + TILE
PACKED = MEMBERS + TILE
F32 = jnp.float32
BF16 = jnp.bfloat16
VMEM_LIMIT = 56 * 1024 * 1024

SMEM_SPEC = pl.BlockSpec(memory_space=pltpu.SMEM)
VMEM_SPEC = pl.BlockSpec(memory_space=pltpu.VMEM)
ANY_SPEC = pl.BlockSpec(memory_space=pl.ANY)


def params():
    return pltpu.CompilerParams(vmem_limit_bytes=VMEM_LIMIT)


def dot_nn(a, b):
    return lax.dot_general(a, b, (((1,), (0,)), ((), ())), preferred_element_type=F32)


def dot_nt(a, b):
    return lax.dot_general(a, b, (((1,), (1,)), ((), ())), preferred_element_type=F32)


def iota(shape, dim):
    return lax.broadcasted_iota(jnp.int32, shape, dim)


def gram_kernel(first, count, lon_size, me_ref, owner_ref, len_ref, points_ref, num_ref,
                weight_ref, innov_ref, taper_ref, pert_ref, *rest):
    outs, (source, filled, rows, w32, i32, t32, built, in_sem, out_sem) = rest[:count], rest[count:]
    held, nobs, _ = pert_ref.shape
    me = me_ref[0]

    @pl.loop(0, lon_size)
    def _(k):
        filled[k] = 0

    @pl.loop(0, count * CAP)
    def _(s):
        source[first * CAP + s] = 0

    @pl.loop(0, held)
    def _(b):
        k = owner_ref[0, b] ^ me
        n = filled[k]
        source[k * CAP + n] = b
        filled[k] = n + 1

    def fetch(step, j):
        b = source[(first + step) * CAP + j]
        return pltpu.make_async_copy(pert_ref.at[b], rows.at[step, j], in_sem.at[step, j])

    @pl.loop(0, count)
    def _(step):
        for j in range(CAP):
            fetch(step, j).start()

    w32[...] = weight_ref[...].astype(F32)
    i32[...] = innov_ref[...].astype(F32)
    t32[...] = jnp.concatenate(
        [taper_ref[...].astype(F32), jnp.zeros((8 - taper_ref.shape[0], held), F32)], axis=0)
    lane_obs = iota((1, nobs), 1)
    lane = iota((1, HALF), 1)
    lane_held = iota((1, held), 1)
    row_id = iota((HALF, HALF), 0)
    col_id = iota((HALF, HALF), 1)

    @pl.loop(0, count)
    def _(step):
        k = first + step
        for j in range(CAP):
            fetch(step, j).wait()
        lo, hi, dg, cf = [], [], [], []
        for j in range(CAP):
            b = source[k * CAP + j]
            present = j < filled[k]
            live = jnp.where(present, len_ref[0, b], 0)
            keep = jnp.where(lane_obs < live, w32[pl.ds(b, 1), :], 0.0)
            pulled = (keep * i32[pl.ds(b, 1), :]).astype(BF16)
            x = rows[step, j]
            scaled = x.T * keep.astype(BF16)
            lhs = jnp.concatenate([scaled, jnp.broadcast_to(pulled, (TILE, nobs))], axis=0)
            gram = dot_nn(lhs, x)
            a11 = gram[0:HALF, 0:HALF]
            a22 = gram[HALF:MEMBERS, HALF:MEMBERS]
            built[step, pl.ds(j * MEMBERS, HALF), :] = jnp.where(row_id <= col_id, a11, a22).astype(BF16)
            built[step, pl.ds(j * MEMBERS + HALF, HALF), :] = gram[0:HALF, HALF:MEMBERS].astype(BF16)
            lo.append(gram[MEMBERS:MEMBERS + 1, 0:HALF])
            hi.append(gram[MEMBERS:MEMBERS + 1, HALF:MEMBERS])
            dg.append(jnp.sum(jnp.where(row_id == col_id, a22, 0.0), axis=0, keepdims=True))
            limit = jnp.where(present, num_ref[b], 0)
            coef = jnp.zeros((1, HALF), F32)
            for q in range(3):
                taper = jnp.sum(jnp.where(lane_held == b, t32[q:q + 1, :], 0.0), axis=1, keepdims=True)
                hit = (lane == points_ref[q, b]) & (q < limit)
                coef = coef + jnp.where(hit, taper, 0.0)
            cf.append(coef)
        built[step, pl.ds(CAP * MEMBERS, TILE), :] = jnp.concatenate(lo + hi + dg + cf, axis=0).astype(BF16)
        for i in range(count):
            @pl.when(step == i)
            def _():
                pltpu.make_async_copy(built.at[i], outs[i], out_sem.at[i]).start()

    for i in range(count):
        pltpu.make_async_copy(built.at[i], outs[i], out_sem.at[i]).wait()


def batch_blocks(first, count, lon_size, me, owner, length, points, num, weight, innov, taper, pert):
    held, nobs, members = pert.shape
    return pl.pallas_call(
        functools.partial(gram_kernel, first, count, lon_size),
        out_shape=[jax.ShapeDtypeStruct((BLOCK, HALF), BF16)] * count,
        in_specs=[SMEM_SPEC] * 5 + [VMEM_SPEC] * 3 + [ANY_SPEC],
        out_specs=[ANY_SPEC] * count,
        scratch_shapes=[
            pltpu.SMEM((lon_size * CAP,), jnp.int32),
            pltpu.SMEM((lon_size,), jnp.int32),
            pltpu.VMEM((count, CAP, nobs, members), BF16),
            pltpu.VMEM((held, nobs), F32),
            pltpu.VMEM((held, nobs), F32),
            pltpu.VMEM((8, held), F32),
            pltpu.VMEM((count, BLOCK, HALF), BF16),
            pltpu.SemaphoreType.DMA((count, CAP)),
            pltpu.SemaphoreType.DMA((count,)),
        ],
        compiler_params=params(),
        cost_estimate=pl.CostEstimate(
            flops=count * CAP * 2 * nobs * members * members,
            bytes_accessed=count * CAP * nobs * members * 2, transcendentals=0),
    )(me, owner, length, points, num, weight, innov, taper, pert)


EDGE = [r * PLON + c for r in range(PLAT) for c in (0, PLON - 1)]
INNER = [r * PLON + c for r in range(PLAT) for c in range(1, PLON - 1)]


def unpack(triangle, corner, diagonal):
    row_id = iota((HALF, HALF), 0)
    col_id = iota((HALF, HALF), 1)
    flipped = triangle.T
    a11 = jnp.where(row_id <= col_id, triangle, flipped)
    a22 = jnp.where(row_id > col_id, triangle, jnp.where(row_id == col_id, diagonal, flipped))
    return jnp.concatenate(
        [jnp.concatenate([a11, corner], axis=1), jnp.concatenate([corner.T, a22], axis=1)], axis=0)


def pack(matrix):
    row_id = iota((HALF, HALF), 0)
    col_id = iota((HALF, HALF), 1)
    a22 = matrix[HALF:MEMBERS, HALF:MEMBERS]
    triangle = jnp.where(row_id <= col_id, matrix[0:HALF, 0:HALF], a22)
    diagonal = jnp.sum(jnp.where(row_id == col_id, a22, 0.0), axis=0, keepdims=True)
    return triangle, matrix[0:HALF, HALF:MEMBERS], diagonal


def sum_by_point(blocks, acc, side):
    slots = len(blocks) * CAP
    extras = [blk[pl.ds(CAP * MEMBERS, TILE), :].astype(F32) for blk in blocks]
    low, high, diag, coef = [
        jnp.concatenate([e[CAP * q:CAP * (q + 1)] for e in extras], axis=0).astype(BF16) for q in range(4)]
    pick = (iota((POINTS, HALF), 0) == iota((POINTS, HALF), 1)).astype(BF16)
    by_point = dot_nt(pick, coef).astype(BF16)
    for q, part in enumerate((diag, low, high)):
        side[q] = dot_nn(by_point, part)
    spread = (iota((POINTS * TILE, HALF), 0) // TILE == iota((POINTS * TILE, HALF), 1)).astype(BF16)
    tall = dot_nt(spread, coef).astype(BF16)
    wide = (iota((slots, slots * TILE), 1) // TILE == iota((slots, slots * TILE), 0)).astype(BF16)
    mixing = dot_nn(tall, wide)
    shape = (POINTS * TILE, slots * TILE)
    mixing = jnp.where(iota(shape, 0) % TILE == iota(shape, 1) % TILE, mixing, 0.0).astype(BF16)
    for g in range(0, MEMBERS // TILE, 2):
        pair = []
        for h in (g, g + 1):
            pair.append(jnp.concatenate(
                [blk[pl.ds(j * MEMBERS + h * TILE, TILE), :] for blk in blocks for j in range(CAP)], axis=0))
        summed = dot_nn(mixing, jnp.concatenate(pair, axis=1))
        for p in range(POINTS):
            for h in (0, 1):
                acc[p, pl.ds((g + h) * TILE, TILE), :] = summed[p * TILE:(p + 1) * TILE, h * HALF:(h + 1) * HALF]


def relay_kernel(count, *refs):
    blocks = refs[:count]
    edge_ref, inner_ref, acc, side = refs[count:]
    sum_by_point(blocks, acc, side)
    for ref, listed in ((edge_ref, EDGE), (inner_ref, INNER)):
        for i, p in enumerate(listed):
            ref[i, pl.ds(0, MEMBERS), :] = acc[p].astype(BF16)
            rows = [side[q, pl.ds(p, 1), :] for q in range(3)] + [jnp.zeros((TILE - 3, HALF), F32)]
            ref[i, pl.ds(MEMBERS, TILE), :] = jnp.concatenate(rows, axis=0).astype(BF16)


def relay_sums(blocks):
    return pl.pallas_call(
        functools.partial(relay_kernel, len(blocks)),
        out_shape=[
            jax.ShapeDtypeStruct((len(EDGE), PACKED, HALF), BF16),
            jax.ShapeDtypeStruct((len(INNER), PACKED, HALF), BF16),
        ],
        in_specs=[VMEM_SPEC] * len(blocks),
        out_specs=[VMEM_SPEC] * 2,
        scratch_shapes=[
            pltpu.VMEM((POINTS, MEMBERS, HALF), F32),
            pltpu.VMEM((3, POINTS, HALF), F32),
        ],
        compiler_params=params(),
        cost_estimate=pl.CostEstimate(
            flops=len(blocks) * CAP * POINTS * TILE * MEMBERS * HALF,
            bytes_accessed=len(blocks) * BLOCK * HALF * 4, transcendentals=0),
    )(*blocks)


def transform_points(listed, total_of, side_of, far_ref, scratch, full_ref, packed_out):
    w32, z32, wb, gb, zb = scratch
    eye = (iota((MEMBERS, MEMBERS), 0) == iota((MEMBERS, MEMBERS), 1)).astype(F32)
    scales, shifts = [], []
    points = range(len(listed))
    for i in points:
        p = listed[i]
        packed = total_of(p) + far_ref[i, pl.ds(0, MEMBERS), :].astype(F32)
        extra = far_ref[i, pl.ds(MEMBERS, TILE), :].astype(F32)
        diagonal, low, high = [side_of(p)[q] + extra[q:q + 1] for q in range(3)]
        shifts.append(jnp.concatenate([low, high], axis=1))
        system = unpack(packed[0:HALF], packed[HALF:MEMBERS], diagonal) + (MEMBERS - 1) * eye
        square = jnp.sum(jnp.sum(system * system, axis=0, keepdims=True), axis=1, keepdims=True)
        inv = lax.rsqrt(square)
        inv = inv * (1.5 - 0.5 * square * inv * inv)
        scales.append(inv)
        iterate = system * inv
        root = 1.5 * eye - 0.5 * iterate
        w32[i] = iterate
        wb[i] = iterate.astype(BF16)
        z32[i] = root
        zb[i] = root.astype(BF16)

    def advance():
        for i in points:
            gb[i] = (0.25 * dot_nn(wb[i], wb[i]) - 1.5 * w32[i]).astype(BF16)
        for i in points:
            value = 2.25 * w32[i] + dot_nn(wb[i], gb[i])
            w32[i] = value
            wb[i] = value.astype(BF16)

    advance()

    @pl.loop(0, ITERS - 2)
    def _(sweep):
        for i in points:
            value = 1.5 * z32[i] - 0.5 * dot_nn(wb[i], zb[i])
            z32[i] = value
            zb[i] = value.astype(BF16)
        advance()

    for i in points:
        z32[i] = 1.5 * z32[i] - 0.5 * dot_nn(wb[i], zb[i])
    for i in points:
        root = z32[i]
        inner = jnp.sum(root * shifts[i], axis=1, keepdims=True)
        mean_weight = jnp.sum(root * inner, axis=0, keepdims=True) * scales[i]
        result = root * jnp.sqrt((MEMBERS - 1) * scales[i])
        full_ref[i] = (result + mean_weight).astype(BF16)
        triangle, corner, diagonal = pack(result)
        extra = jnp.concatenate(
            [diagonal, mean_weight[:, 0:HALF], mean_weight[:, HALF:MEMBERS], jnp.zeros((TILE - 3, HALF), F32)],
            axis=0)
        ref, where = packed_out(listed[i])
        ref[where, pl.ds(0, HALF), :] = triangle.astype(BF16)
        ref[where, pl.ds(HALF, HALF), :] = corner.astype(BF16)
        ref[where, pl.ds(MEMBERS, TILE), :] = extra.astype(BF16)


def edge_kernel(count, *refs):
    blocks = refs[:count]
    far_ref, left_ref, right_ref, full_ref, total_ref, side_ref, w32, z32, wb, gb, zb, acc = refs[count:]
    sum_by_point(blocks, acc, side_ref)
    for i, p in enumerate(INNER):
        total_ref[i] = acc[p]
    transform_points(
        EDGE,
        lambda p: acc[p],
        lambda p: [side_ref[q, pl.ds(p, 1), :] for q in range(3)],
        far_ref, (w32, z32, wb, gb, zb), full_ref,
        lambda p: (left_ref if p % PLON == 0 else right_ref, p // PLON))


def inner_kernel(total_in, side_in, far_ref, left_ref, right_ref, full_ref, *refs):
    rows, scratch = refs[:PLAT], refs[PLAT:]
    transform_points(
        INNER,
        lambda p: total_in[INNER.index(p)],
        lambda p: [side_in[q, pl.ds(p, 1), :] for q in range(3)],
        far_ref, scratch, full_ref,
        lambda p: (rows[p // PLON], p % PLON + 1))
    for r in range(PLAT):
        rows[r][1] = left_ref[r]
        rows[r][PLON] = right_ref[r]


def newton_scratch(count):
    shape = (count, MEMBERS, MEMBERS)
    return [pltpu.VMEM(shape, F32)] * 2 + [pltpu.VMEM(shape, BF16)] * 3


def edge_transforms(blocks, far):
    columns = jax.ShapeDtypeStruct((PLAT, PACKED, HALF), BF16)
    return pl.pallas_call(
        functools.partial(edge_kernel, len(blocks)),
        out_shape=[
            columns, columns,
            jax.ShapeDtypeStruct((len(EDGE), MEMBERS, MEMBERS), BF16),
            jax.ShapeDtypeStruct((len(INNER), MEMBERS, HALF), F32),
            jax.ShapeDtypeStruct((3, POINTS, HALF), F32),
        ],
        in_specs=[VMEM_SPEC] * (len(blocks) + 1),
        out_specs=[VMEM_SPEC] * 5,
        scratch_shapes=newton_scratch(len(EDGE)) + [pltpu.VMEM((POINTS, MEMBERS, HALF), F32)],
        compiler_params=params(),
        cost_estimate=pl.CostEstimate(
            flops=len(EDGE) * 15 * 2 * MEMBERS ** 3, bytes_accessed=8 * MEMBERS * HALF * 6, transcendentals=0),
    )(*blocks, far)


def inner_transforms(total, side, far, left, right):
    count = total.shape[0]
    row = jax.ShapeDtypeStruct((PLON + 2, PACKED, HALF), BF16)
    return pl.pallas_call(
        inner_kernel,
        out_shape=[jax.ShapeDtypeStruct((count, MEMBERS, MEMBERS), BF16)] + [row] * PLAT,
        in_specs=[VMEM_SPEC] * 5,
        out_specs=[VMEM_SPEC] * (1 + PLAT),
        scratch_shapes=newton_scratch(count),
        compiler_params=params(),
        cost_estimate=pl.CostEstimate(
            flops=count * 15 * 2 * MEMBERS ** 3, bytes_accessed=count * MEMBERS * HALF * 6, transcendentals=0),
    )(total, side, far, left, right)


WIDE = PLON + 2
WINDOW = (PLAT + 2) * WIDE
MID = list(range(WIDE, WINDOW - WIDE))
RIM = list(range(WIDE)) + list(range(WINDOW - WIDE, WINDOW))


def cell_kernel(point_cols, pos_ref, stencil_ref, frac_ref, field_ref, mid_ref, rim_ref, mean_ref):
    width = stencil_ref.shape[2]
    lat_pos, lon_pos = pos_ref[0], pos_ref[1]
    i = pl.program_id(0)
    ids = iota((HALF, width), 0)
    field = field_ref[0].astype(F32)
    mean = jnp.mean(field, axis=1, keepdims=True)
    mean_ref[...] = jnp.broadcast_to(mean, mean_ref.shape)
    dev = (field - mean).astype(BF16).astype(F32)
    row_off = stencil_ref[0, pl.ds(i, 1), :] - (lat_pos * PLAT - 1)
    col_off = stencil_ref[1, pl.ds(i, 1), :] - (lon_pos * PLON - 1)
    col_off = jnp.where(col_off < 0, col_off + point_cols, col_off)
    col_off = jnp.where(col_off >= point_cols, col_off - point_cols, col_off)
    y = frac_ref[0, pl.ds(i, 1), :]
    x = frac_ref[1, pl.ds(i, 1), :]
    corner = row_off * WIDE + col_off
    weights = jnp.where(corner == ids, (1.0 - y) * (1.0 - x), 0.0)
    weights = weights + jnp.where(corner + WIDE == ids, y * (1.0 - x), 0.0)
    weights = weights + jnp.where(corner + 1 == ids, (1.0 - y) * x, 0.0)
    weights = weights + jnp.where(corner + WIDE + 1 == ids, y * x, 0.0)
    turned = weights.T
    for ref, listed in ((mid_ref, MID), (rim_ref, RIM)):
        for n, point in enumerate(listed):
            ref[:, n * MEMBERS:(n + 1) * MEMBERS] = (dev * turned[:, point:point + 1]).astype(BF16)


def cell_parts(point_cols, pos, stencil, frac, background):
    rows, width, members = background.shape
    cells = rows * width
    return pl.pallas_call(
        functools.partial(cell_kernel, point_cols),
        grid=(rows,),
        out_shape=[
            jax.ShapeDtypeStruct((cells, len(MID) * members), BF16),
            jax.ShapeDtypeStruct((cells, len(RIM) * members), BF16),
            jax.ShapeDtypeStruct((cells, HALF), F32),
        ],
        in_specs=[
            SMEM_SPEC,
            pl.BlockSpec(stencil.shape, lambda i: (0, 0, 0)),
            pl.BlockSpec(frac.shape, lambda i: (0, 0, 0)),
            pl.BlockSpec((1, width, members), lambda i: (i, 0, 0)),
        ],
        out_specs=[
            pl.BlockSpec((width, len(MID) * members), lambda i: (i, 0)),
            pl.BlockSpec((width, len(RIM) * members), lambda i: (i, 0)),
            pl.BlockSpec((width, HALF), lambda i: (i, 0)),
        ],
        compiler_params=params(),
        cost_estimate=pl.CostEstimate(
            flops=cells * members * WINDOW, bytes_accessed=cells * members * (2 * WINDOW + 4), transcendentals=0),
    )(pos, stencil, frac, background)


def place_packed(matrices, slot, ref, i):
    extra = ref[i, pl.ds(MEMBERS, TILE), :].astype(F32)
    full = unpack(ref[i, pl.ds(0, HALF), :].astype(F32), ref[i, pl.ds(HALF, HALF), :].astype(F32), extra[0:1])
    full = full + jnp.concatenate([extra[1:2], extra[2:3]], axis=1)
    matrices[:, slot * MEMBERS:(slot + 1) * MEMBERS] = full.astype(BF16)


def mid_kernel(before, after, edge, inner, lhs_ref, mean_ref, out_ref, matrices):
    @pl.when(pl.program_id(0) == 0)
    def _():
        for r in range(PLAT):
            place_packed(matrices, r * WIDE, before, r)
            place_packed(matrices, r * WIDE + PLON + 1, after, r)
            for c in range(PLON):
                p = r * PLON + c
                value = edge[EDGE.index(p)] if p in EDGE else inner[INNER.index(p)]
                slot = r * WIDE + c + 1
                matrices[:, slot * MEMBERS:(slot + 1) * MEMBERS] = value

    out_ref[...] = dot_nt(lhs_ref[...], matrices[...]) + mean_ref[:, 0:1]


def rim_kernel(above, below, lhs_ref, base_ref, out_ref, matrices):
    @pl.when(pl.program_id(0) == 0)
    def _():
        for c in range(WIDE):
            place_packed(matrices, c, above, c)
            place_packed(matrices, WIDE + c, below, c)

    out_ref[...] = (dot_nt(lhs_ref[...], matrices[...]) + base_ref[...]).astype(BF16)


def mix(kernel, transforms, lhs, base, dtype):
    cells, depth = lhs.shape
    tile = min(cells, 2 * MEMBERS)
    return pl.pallas_call(
        kernel,
        grid=(cells // tile,),
        out_shape=jax.ShapeDtypeStruct((cells, MEMBERS), dtype),
        in_specs=[pl.BlockSpec(t.shape, lambda i: (0, 0, 0)) for t in transforms] + [
            pl.BlockSpec((tile, depth), lambda i: (i, 0)),
            pl.BlockSpec((tile, base.shape[1]), lambda i: (i, 0)),
        ],
        out_specs=pl.BlockSpec((tile, MEMBERS), lambda i: (i, 0)),
        scratch_shapes=[pltpu.VMEM((MEMBERS, depth), BF16)],
        compiler_params=params(),
        cost_estimate=pl.CostEstimate(
            flops=2 * cells * depth * MEMBERS, bytes_accessed=cells * depth * 2, transcendentals=0),
    )(*transforms, lhs, base)


def on_device(obs_pert, obs_weight, innovation, batch_len, batch_owner, batch_points, batch_count,
              batch_taper, background, stencil, frac):
    lon_size, lat_size = lax.axis_size("lon"), lax.axis_size("lat")
    lat_pos, lon_pos = lax.axis_index("lat"), lax.axis_index("lon")
    me = lon_pos.astype(jnp.int32).reshape(1)
    pos = jnp.stack([lat_pos, lon_pos]).astype(jnp.int32)
    fixed = (me, batch_owner.T, batch_len, batch_points.T, batch_count, obs_weight, innovation, batch_taper.T,
             obs_pert)
    half = lon_size // 2

    def swap(value, offset):
        return lax.ppermute(value, "lon", [(i, i ^ offset) for i in range(lon_size)])

    far = batch_blocks(half, half, lon_size, *fixed)
    relayed = [far[0]] + [swap(far[i], i) for i in range(1, half)]
    near = batch_blocks(0, half, lon_size, *fixed)
    got = [near[0]] + [swap(near[i], i) for i in range(1, half)]
    relayed, _ = lax.optimization_barrier((relayed, near))
    far_edge, far_inner = relay_sums(relayed)
    far_edge, far_inner, background = lax.optimization_barrier((far_edge, far_inner, background))
    mid_lhs, rim_lhs, mean = cell_parts(PLON * lon_size, pos, stencil, frac, background)
    far_edge = swap(far_edge, half)
    far_inner, got, mid_lhs, rim_lhs, mean = lax.optimization_barrier((far_inner, got, mid_lhs, rim_lhs, mean))
    far_inner = swap(far_inner, half)

    left, right, edge, total, side = edge_transforms(got, far_edge)
    up = [(i, (i + 1) % lon_size) for i in range(lon_size)]
    down = [(j, i) for i, j in up]
    before = lax.ppermute(right, "lon", up)
    after = lax.ppermute(left, "lon", down)
    inner, *rows = inner_transforms(total, side, far_inner, left, right)
    rows = [rows[r].at[0].set(before[r]).at[PLON + 1].set(after[r]) for r in range(PLAT)]
    north = [(i, i + 1) for i in range(lat_size - 1)]
    south = [(j, i) for i, j in north]
    above = lax.ppermute(rows[PLAT - 1], "lat", north)
    below = lax.ppermute(rows[0], "lat", south)
    partial = mix(mid_kernel, [before, after, edge, inner], mid_lhs, mean, F32)
    return mix(rim_kernel, [above, below], rim_lhs, partial, BF16).reshape(background.shape)


def solution(mesh):
    return jax.shard_map(
        on_device,
        mesh=mesh,
        in_specs=(
            P(("lat", "lon"), None, None),
            P(("lat", "lon"), None),
            P(("lat", "lon"), None),
            P(("lat", "lon"), None),
            P(("lat", "lon"), None),
            P(("lat", "lon"), None),
            P(("lat", "lon")),
            P(("lat", "lon"), None),
            P("lat", "lon", None),
            P(None, "lat", "lon"),
            P(None, "lat", "lon"),
        ),
        out_specs=P("lat", "lon", None),
        check_vma=False,
    )
```

```python
import functools

import jax
import jax.numpy as jnp
from jax import lax
from jax.experimental import pallas as pl
from jax.experimental.pallas import tpu as pltpu
from jax.sharding import PartitionSpec as P

CAP = 4
PLAT = 2
PLON = 4
POINTS = PLAT * PLON
ITERS = 6
HALF = 128
MEMBERS = 2 * HALF
TILE = 16
BLOCK = CAP * MEMBERS + TILE
PACKED = MEMBERS + TILE
F32 = jnp.float32
BF16 = jnp.bfloat16
MIB = 1024 * 1024

SMEM_SPEC = pl.BlockSpec(memory_space=pltpu.SMEM)
VMEM_SPEC = pl.BlockSpec(memory_space=pltpu.VMEM)
ANY_SPEC = pl.BlockSpec(memory_space=pl.ANY)


def params(mebibytes):
    return pltpu.CompilerParams(vmem_limit_bytes=mebibytes * MIB)


def dot_nn(a, b):
    return lax.dot_general(a, b, (((1,), (0,)), ((), ())), preferred_element_type=F32)


def dot_nt(a, b):
    return lax.dot_general(a, b, (((1,), (1,)), ((), ())), preferred_element_type=F32)


def iota(shape, dim):
    return lax.broadcasted_iota(jnp.int32, shape, dim)


def gram_kernel(first, count, lon_size, me_ref, *refs):
    owner_hbm, len_hbm, points_hbm, num_hbm, weight_hbm, innov_hbm, taper_hbm, pert_ref = refs[:8]
    outs = refs[8:8 + count]
    (owner_ref, len_ref, points_ref, num_ref, weight_ref, innov_ref, taper_ref,
     source, filled, rows, w32, i32, t32, built, small_sem, in_sem, out_sem) = refs[8 + count:]
    held, nobs, _ = pert_ref.shape
    me = me_ref[0]
    loads = [
        pltpu.make_async_copy(a, b, small_sem.at[n])
        for n, (a, b) in enumerate((
            (owner_hbm, owner_ref), (len_hbm, len_ref), (points_hbm, points_ref), (num_hbm, num_ref),
            (weight_hbm, weight_ref), (innov_hbm, innov_ref), (taper_hbm, taper_ref)))]
    for load in loads:
        load.start()

    @pl.loop(0, lon_size)
    def _(k):
        filled[k] = 0

    @pl.loop(0, count * CAP)
    def _(s):
        source[first * CAP + s] = 0

    loads[0].wait()

    @pl.loop(0, held)
    def _(b):
        k = owner_ref[0, b] ^ me
        n = filled[k]
        source[k * CAP + n] = b
        filled[k] = n + 1

    def fetch(step, j):
        b = source[(first + step) * CAP + j]
        return pltpu.make_async_copy(pert_ref.at[b], rows.at[step, j], in_sem.at[step, j])

    @pl.loop(0, count)
    def _(step):
        for j in range(CAP):
            fetch(step, j).start()

    for load in loads[1:]:
        load.wait()
    w32[...] = weight_ref[...].astype(F32)
    i32[...] = innov_ref[...].astype(F32)
    t32[...] = jnp.concatenate(
        [taper_ref[...].astype(F32), jnp.zeros((8 - taper_ref.shape[0], held), F32)], axis=0)
    lane_obs = iota((1, nobs), 1)
    lane = iota((1, HALF), 1)
    lane_held = iota((1, held), 1)
    row_id = iota((HALF, HALF), 0)
    col_id = iota((HALF, HALF), 1)

    @pl.loop(0, count)
    def _(step):
        k = first + step
        for j in range(CAP):
            fetch(step, j).wait()
        lo, hi, dg, cf = [], [], [], []
        for j in range(CAP):
            b = source[k * CAP + j]
            present = j < filled[k]
            live = jnp.where(present, len_ref[0, b], 0)
            keep = jnp.where(lane_obs < live, w32[pl.ds(b, 1), :], 0.0)
            pulled = (keep * i32[pl.ds(b, 1), :]).astype(BF16)
            x = rows[step, j]
            scaled = x.T * keep.astype(BF16)
            lhs = jnp.concatenate([scaled, jnp.broadcast_to(pulled, (TILE, nobs))], axis=0)
            gram = dot_nn(lhs, x)
            a11 = gram[0:HALF, 0:HALF]
            a22 = gram[HALF:MEMBERS, HALF:MEMBERS]
            built[step, pl.ds(j * MEMBERS, HALF), :] = jnp.where(row_id <= col_id, a11, a22).astype(BF16)
            built[step, pl.ds(j * MEMBERS + HALF, HALF), :] = gram[0:HALF, HALF:MEMBERS].astype(BF16)
            lo.append(gram[MEMBERS:MEMBERS + 1, 0:HALF])
            hi.append(gram[MEMBERS:MEMBERS + 1, HALF:MEMBERS])
            dg.append(jnp.sum(jnp.where(row_id == col_id, a22, 0.0), axis=0, keepdims=True))
            limit = jnp.where(present, num_ref[b], 0)
            coef = jnp.zeros((1, HALF), F32)
            for q in range(3):
                taper = jnp.sum(jnp.where(lane_held == b, t32[q:q + 1, :], 0.0), axis=1, keepdims=True)
                hit = (lane == points_ref[q, b]) & (q < limit)
                coef = coef + jnp.where(hit, taper, 0.0)
            cf.append(coef)
        built[step, pl.ds(CAP * MEMBERS, TILE), :] = jnp.concatenate(lo + hi + dg + cf, axis=0).astype(BF16)
        for i in range(count):
            @pl.when(step == i)
            def _():
                pltpu.make_async_copy(built.at[i], outs[i], out_sem.at[i]).start()

    for i in range(count):
        pltpu.make_async_copy(built.at[i], outs[i], out_sem.at[i]).wait()


def batch_blocks(room, first, count, lon_size, me, owner, length, points, num, weight, innov, taper, pert):
    held, nobs, members = pert.shape
    return pl.pallas_call(
        functools.partial(gram_kernel, first, count, lon_size),
        out_shape=[jax.ShapeDtypeStruct((BLOCK, HALF), BF16)] * count,
        in_specs=[SMEM_SPEC] + [ANY_SPEC] * 8,
        out_specs=[ANY_SPEC] * count,
        scratch_shapes=[
            pltpu.SMEM(owner.shape, jnp.int32),
            pltpu.SMEM(length.shape, jnp.int32),
            pltpu.SMEM(points.shape, jnp.int32),
            pltpu.SMEM(num.shape, jnp.int32),
            pltpu.VMEM(weight.shape, BF16),
            pltpu.VMEM(innov.shape, BF16),
            pltpu.VMEM(taper.shape, BF16),
            pltpu.SMEM((lon_size * CAP,), jnp.int32),
            pltpu.SMEM((lon_size,), jnp.int32),
            pltpu.VMEM((count, CAP, nobs, members), BF16),
            pltpu.VMEM((held, nobs), F32),
            pltpu.VMEM((held, nobs), F32),
            pltpu.VMEM((8, held), F32),
            pltpu.VMEM((count, BLOCK, HALF), BF16),
            pltpu.SemaphoreType.DMA((7,)),
            pltpu.SemaphoreType.DMA((count, CAP)),
            pltpu.SemaphoreType.DMA((count,)),
        ],
        compiler_params=params(room),
        cost_estimate=pl.CostEstimate(
            flops=count * CAP * 2 * nobs * members * members,
            bytes_accessed=count * CAP * nobs * members * 2, transcendentals=0),
    )(me, owner, length, points, num, weight, innov, taper, pert)


EDGE = [r * PLON + c for r in range(PLAT) for c in (0, PLON - 1)]
INNER = [r * PLON + c for r in range(PLAT) for c in range(1, PLON - 1)]


def unpack(triangle, corner, diagonal):
    row_id = iota((HALF, HALF), 0)
    col_id = iota((HALF, HALF), 1)
    flipped = triangle.T
    a11 = jnp.where(row_id <= col_id, triangle, flipped)
    a22 = jnp.where(row_id > col_id, triangle, jnp.where(row_id == col_id, diagonal, flipped))
    return jnp.concatenate(
        [jnp.concatenate([a11, corner], axis=1), jnp.concatenate([corner.T, a22], axis=1)], axis=0)


def pack(matrix):
    row_id = iota((HALF, HALF), 0)
    col_id = iota((HALF, HALF), 1)
    a22 = matrix[HALF:MEMBERS, HALF:MEMBERS]
    triangle = jnp.where(row_id <= col_id, matrix[0:HALF, 0:HALF], a22)
    diagonal = jnp.sum(jnp.where(row_id == col_id, a22, 0.0), axis=0, keepdims=True)
    return triangle, matrix[0:HALF, HALF:MEMBERS], diagonal


def sum_by_point(blocks, acc, side):
    slots = len(blocks) * CAP
    extras = [blk[pl.ds(CAP * MEMBERS, TILE), :].astype(F32) for blk in blocks]
    low, high, diag, coef = [
        jnp.concatenate([e[CAP * q:CAP * (q + 1)] for e in extras], axis=0).astype(BF16) for q in range(4)]
    pick = (iota((POINTS, HALF), 0) == iota((POINTS, HALF), 1)).astype(BF16)
    by_point = dot_nt(pick, coef).astype(BF16)
    for q, part in enumerate((diag, low, high)):
        side[q] = dot_nn(by_point, part)
    spread = (iota((POINTS * TILE, HALF), 0) // TILE == iota((POINTS * TILE, HALF), 1)).astype(BF16)
    tall = dot_nt(spread, coef).astype(BF16)
    wide = (iota((slots, slots * TILE), 1) // TILE == iota((slots, slots * TILE), 0)).astype(BF16)
    mixing = dot_nn(tall, wide)
    shape = (POINTS * TILE, slots * TILE)
    mixing = jnp.where(iota(shape, 0) % TILE == iota(shape, 1) % TILE, mixing, 0.0).astype(BF16)
    for g in range(0, MEMBERS // TILE, 2):
        pair = []
        for h in (g, g + 1):
            pair.append(jnp.concatenate(
                [blk[pl.ds(j * MEMBERS + h * TILE, TILE), :] for blk in blocks for j in range(CAP)], axis=0))
        summed = dot_nn(mixing, jnp.concatenate(pair, axis=1))
        for p in range(POINTS):
            for h in (0, 1):
                acc[p, pl.ds((g + h) * TILE, TILE), :] = summed[p * TILE:(p + 1) * TILE, h * HALF:(h + 1) * HALF]


def relay_kernel(count, *refs):
    blocks = refs[:count]
    edge_ref, inner_ref, acc, side = refs[count:]
    sum_by_point(blocks, acc, side)
    for ref, listed in ((edge_ref, EDGE), (inner_ref, INNER)):
        for i, p in enumerate(listed):
            ref[i, pl.ds(0, MEMBERS), :] = acc[p].astype(BF16)
            rows = [side[q, pl.ds(p, 1), :] for q in range(3)] + [jnp.zeros((TILE - 3, HALF), F32)]
            ref[i, pl.ds(MEMBERS, TILE), :] = jnp.concatenate(rows, axis=0).astype(BF16)


def relay_sums(blocks):
    return pl.pallas_call(
        functools.partial(relay_kernel, len(blocks)),
        out_shape=[
            jax.ShapeDtypeStruct((len(EDGE), PACKED, HALF), BF16),
            jax.ShapeDtypeStruct((len(INNER), PACKED, HALF), BF16),
        ],
        in_specs=[VMEM_SPEC] * len(blocks),
        out_specs=[VMEM_SPEC] * 2,
        scratch_shapes=[
            pltpu.VMEM((POINTS, MEMBERS, HALF), F32),
            pltpu.VMEM((3, POINTS, HALF), F32),
        ],
        compiler_params=params(6 + len(blocks)),
        cost_estimate=pl.CostEstimate(
            flops=len(blocks) * CAP * POINTS * TILE * MEMBERS * HALF,
            bytes_accessed=len(blocks) * BLOCK * HALF * 4, transcendentals=0),
    )(*blocks)


def transform_points(listed, total_of, side_of, far_ref, scratch, full_ref, packed_out):
    w32, z32, wb, gb, zb = scratch
    eye = (iota((MEMBERS, MEMBERS), 0) == iota((MEMBERS, MEMBERS), 1)).astype(F32)
    scales, shifts = [], []
    points = range(len(listed))
    for i in points:
        p = listed[i]
        packed = total_of(p) + far_ref[i, pl.ds(0, MEMBERS), :].astype(F32)
        extra = far_ref[i, pl.ds(MEMBERS, TILE), :].astype(F32)
        diagonal, low, high = [side_of(p)[q] + extra[q:q + 1] for q in range(3)]
        shifts.append(jnp.concatenate([low, high], axis=1))
        system = unpack(packed[0:HALF], packed[HALF:MEMBERS], diagonal) + (MEMBERS - 1) * eye
        square = jnp.sum(jnp.sum(system * system, axis=0, keepdims=True), axis=1, keepdims=True)
        inv = lax.rsqrt(square)
        inv = inv * (1.5 - 0.5 * square * inv * inv)
        scales.append(inv)
        iterate = system * inv
        root = 1.5 * eye - 0.5 * iterate
        w32[i] = iterate
        wb[i] = iterate.astype(BF16)
        z32[i] = root
        zb[i] = root.astype(BF16)

    def advance():
        for i in points:
            gb[i] = (0.25 * dot_nn(wb[i], wb[i]) - 1.5 * w32[i]).astype(BF16)
        for i in points:
            value = 2.25 * w32[i] + dot_nn(wb[i], gb[i])
            w32[i] = value
            wb[i] = value.astype(BF16)

    advance()

    @pl.loop(0, ITERS - 2)
    def _(sweep):
        for i in points:
            value = 1.5 * z32[i] - 0.5 * dot_nn(wb[i], zb[i])
            z32[i] = value
            zb[i] = value.astype(BF16)
        advance()

    for i in points:
        z32[i] = 1.5 * z32[i] - 0.5 * dot_nn(wb[i], zb[i])
    for i in points:
        root = z32[i]
        inner = jnp.sum(root * shifts[i], axis=1, keepdims=True)
        mean_weight = jnp.sum(root * inner, axis=0, keepdims=True) * scales[i]
        result = root * jnp.sqrt((MEMBERS - 1) * scales[i])
        column = jnp.broadcast_to(mean_weight, (HALF, MEMBERS)).T
        full_ref[i] = (result + jnp.concatenate([column, column], axis=1)).astype(BF16)
        triangle, corner, diagonal = pack(result)
        extra = jnp.concatenate(
            [diagonal, mean_weight[:, 0:HALF], mean_weight[:, HALF:MEMBERS], jnp.zeros((TILE - 3, HALF), F32)],
            axis=0)
        ref, where = packed_out(listed[i])
        ref[where, pl.ds(0, HALF), :] = triangle.astype(BF16)
        ref[where, pl.ds(HALF, HALF), :] = corner.astype(BF16)
        ref[where, pl.ds(MEMBERS, TILE), :] = extra.astype(BF16)


def edge_kernel(count, *refs):
    blocks = refs[:count]
    far_ref, left_ref, right_ref, full_ref, total_ref, side_ref, w32, z32, wb, gb, zb, acc = refs[count:]
    sum_by_point(blocks, acc, side_ref)
    for i, p in enumerate(INNER):
        total_ref[i] = acc[p]
    transform_points(
        EDGE,
        lambda p: acc[p],
        lambda p: [side_ref[q, pl.ds(p, 1), :] for q in range(3)],
        far_ref, (w32, z32, wb, gb, zb), full_ref,
        lambda p: (left_ref if p % PLON == 0 else right_ref, p // PLON))


def inner_kernel(total_in, side_in, far_ref, left_ref, right_ref, full_ref, *refs):
    rows, scratch = refs[:PLAT], refs[PLAT:]
    transform_points(
        INNER,
        lambda p: total_in[INNER.index(p)],
        lambda p: [side_in[q, pl.ds(p, 1), :] for q in range(3)],
        far_ref, scratch, full_ref,
        lambda p: (rows[p // PLON], p % PLON + 1))
    for r in range(PLAT):
        rows[r][1] = left_ref[r]
        rows[r][PLON] = right_ref[r]


def newton_scratch(count):
    shape = (count, MEMBERS, MEMBERS)
    return [pltpu.VMEM(shape, F32)] * 2 + [pltpu.VMEM(shape, BF16)] * 3


def edge_transforms(blocks, far):
    columns = jax.ShapeDtypeStruct((PLAT, PACKED, HALF), BF16)
    return pl.pallas_call(
        functools.partial(edge_kernel, len(blocks)),
        out_shape=[
            columns, columns,
            jax.ShapeDtypeStruct((len(EDGE), MEMBERS, MEMBERS), BF16),
            jax.ShapeDtypeStruct((len(INNER), MEMBERS, HALF), F32),
            jax.ShapeDtypeStruct((3, POINTS, HALF), F32),
        ],
        in_specs=[VMEM_SPEC] * (len(blocks) + 1),
        out_specs=[VMEM_SPEC] * 5,
        scratch_shapes=newton_scratch(len(EDGE)) + [pltpu.VMEM((POINTS, MEMBERS, HALF), F32)],
        compiler_params=params(12 + len(blocks)),
        cost_estimate=pl.CostEstimate(
            flops=len(EDGE) * 15 * 2 * MEMBERS ** 3, bytes_accessed=8 * MEMBERS * HALF * 6, transcendentals=0),
    )(*blocks, far)


def inner_transforms(total, side, far, left, right):
    count = total.shape[0]
    row = jax.ShapeDtypeStruct((PLON + 2, PACKED, HALF), BF16)
    return pl.pallas_call(
        inner_kernel,
        out_shape=[jax.ShapeDtypeStruct((count, MEMBERS, MEMBERS), BF16)] + [row] * PLAT,
        in_specs=[VMEM_SPEC] * 5,
        out_specs=[VMEM_SPEC] * (1 + PLAT),
        scratch_shapes=newton_scratch(count),
        compiler_params=params(12),
        cost_estimate=pl.CostEstimate(
            flops=count * 15 * 2 * MEMBERS ** 3, bytes_accessed=count * MEMBERS * HALF * 6, transcendentals=0),
    )(total, side, far, left, right)


WIDE = PLON + 2
WINDOW = (PLAT + 2) * WIDE
MID = list(range(WIDE, WINDOW - WIDE))
RIM = list(range(WIDE)) + list(range(WINDOW - WIDE, WINDOW))


def cell_kernel(point_cols, pos_ref, stencil_ref, frac_ref, field_ref, mid_ref, rim_ref, mean_ref):
    width = stencil_ref.shape[2]
    lat_pos, lon_pos = pos_ref[0], pos_ref[1]
    i = pl.program_id(0)
    ids = iota((HALF, width), 0)
    field = field_ref[0].astype(F32)
    mean = jnp.mean(field, axis=1, keepdims=True)
    mean_ref[...] = jnp.broadcast_to(mean, mean_ref.shape)
    dev = (field - mean).astype(BF16).astype(F32)
    row_off = stencil_ref[0, pl.ds(i, 1), :] - (lat_pos * PLAT - 1)
    col_off = stencil_ref[1, pl.ds(i, 1), :] - (lon_pos * PLON - 1)
    col_off = jnp.where(col_off < 0, col_off + point_cols, col_off)
    col_off = jnp.where(col_off >= point_cols, col_off - point_cols, col_off)
    y = frac_ref[0, pl.ds(i, 1), :]
    x = frac_ref[1, pl.ds(i, 1), :]
    corner = row_off * WIDE + col_off
    weights = jnp.where(corner == ids, (1.0 - y) * (1.0 - x), 0.0)
    weights = weights + jnp.where(corner + WIDE == ids, y * (1.0 - x), 0.0)
    weights = weights + jnp.where(corner + 1 == ids, (1.0 - y) * x, 0.0)
    weights = weights + jnp.where(corner + WIDE + 1 == ids, y * x, 0.0)
    turned = weights.T
    for ref, listed in ((mid_ref, MID), (rim_ref, RIM)):
        for n, point in enumerate(listed):
            ref[:, n * MEMBERS:(n + 1) * MEMBERS] = (dev * turned[:, point:point + 1]).astype(BF16)


def cell_parts(point_cols, pos, stencil, frac, background):
    rows, width, members = background.shape
    cells = rows * width
    return pl.pallas_call(
        functools.partial(cell_kernel, point_cols),
        grid=(rows,),
        out_shape=[
            jax.ShapeDtypeStruct((cells, len(MID) * members), BF16),
            jax.ShapeDtypeStruct((cells, len(RIM) * members), BF16),
            jax.ShapeDtypeStruct((cells, HALF), F32),
        ],
        in_specs=[
            SMEM_SPEC,
            pl.BlockSpec(stencil.shape, lambda i: (0, 0, 0)),
            pl.BlockSpec(frac.shape, lambda i: (0, 0, 0)),
            pl.BlockSpec((1, width, members), lambda i: (i, 0, 0)),
        ],
        out_specs=[
            pl.BlockSpec((width, len(MID) * members), lambda i: (i, 0)),
            pl.BlockSpec((width, len(RIM) * members), lambda i: (i, 0)),
            pl.BlockSpec((width, HALF), lambda i: (i, 0)),
        ],
        compiler_params=params(12),
        cost_estimate=pl.CostEstimate(
            flops=cells * members * WINDOW, bytes_accessed=cells * members * (2 * WINDOW + 4), transcendentals=0),
    )(pos, stencil, frac, background)


def place_packed(matrices, slot, ref, i):
    extra = ref[i, pl.ds(MEMBERS, TILE), :].astype(F32)
    full = unpack(ref[i, pl.ds(0, HALF), :].astype(F32), ref[i, pl.ds(HALF, HALF), :].astype(F32), extra[0:1])
    row = jnp.concatenate([extra[1:2], extra[2:3]], axis=1)
    column = jnp.broadcast_to(row, (HALF, MEMBERS)).T
    full = full + jnp.concatenate([column, column], axis=1)
    matrices[pl.ds(slot * MEMBERS, MEMBERS), :] = full.astype(BF16)


def mid_kernel(before, after, edge, inner, lhs_ref, mean_ref, out_ref, matrices):
    for r in range(PLAT):
        place_packed(matrices, r * WIDE, before, r)
        place_packed(matrices, r * WIDE + PLON + 1, after, r)
        for c in range(PLON):
            p = r * PLON + c
            value = edge[EDGE.index(p)] if p in EDGE else inner[INNER.index(p)]
            matrices[pl.ds((r * WIDE + c + 1) * MEMBERS, MEMBERS), :] = value

    @pl.loop(0, lhs_ref.shape[0] // MEMBERS)
    def _(t):
        at = pl.ds(t * MEMBERS, MEMBERS)
        out_ref[at, :] = dot_nn(lhs_ref[at, :], matrices[...]) + mean_ref[at, 0:1]


def rim_kernel(above, below, lhs_ref, base_ref, out_ref, matrices):
    for c in range(WIDE):
        place_packed(matrices, c, above, c)
        place_packed(matrices, WIDE + c, below, c)

    @pl.loop(0, lhs_ref.shape[0] // MEMBERS)
    def _(t):
        at = pl.ds(t * MEMBERS, MEMBERS)
        out_ref[at, :] = (dot_nn(lhs_ref[at, :], matrices[...]) + base_ref[at, :]).astype(BF16)


def mix(kernel, transforms, lhs, base, dtype):
    cells, depth = lhs.shape
    return pl.pallas_call(
        kernel,
        out_shape=jax.ShapeDtypeStruct((cells, MEMBERS), dtype),
        in_specs=[VMEM_SPEC] * (len(transforms) + 2),
        out_specs=VMEM_SPEC,
        scratch_shapes=[pltpu.VMEM((depth, MEMBERS), BF16)],
        compiler_params=params(20),
        cost_estimate=pl.CostEstimate(
            flops=2 * cells * depth * MEMBERS, bytes_accessed=cells * depth * 2, transcendentals=0),
    )(*transforms, lhs, base)


def on_device(obs_pert, obs_weight, innovation, batch_len, batch_owner, batch_points, batch_count,
              batch_taper, background, stencil, frac):
    lon_size, lat_size = lax.axis_size("lon"), lax.axis_size("lat")
    lat_pos, lon_pos = lax.axis_index("lat"), lax.axis_index("lon")
    me = lon_pos.astype(jnp.int32).reshape(1)
    pos = jnp.stack([lat_pos, lon_pos]).astype(jnp.int32)
    fixed = (me, batch_owner.T, batch_len, batch_points.T, batch_count, obs_weight, innovation, batch_taper.T,
             obs_pert)
    half = lon_size // 2

    def swap(value, offset):
        return lax.ppermute(value, "lon", [(i, i ^ offset) for i in range(lon_size)])

    far = batch_blocks(57, half, half, lon_size, *fixed)
    relayed = [far[0]] + [swap(far[i], i) for i in range(1, half)]
    near = batch_blocks(57, 0, half, lon_size, *fixed)
    got = [near[0]] + [swap(near[i], i) for i in range(1, half)]
    relayed, _ = lax.optimization_barrier((relayed, near))
    far_edge, far_inner = relay_sums(relayed)
    far_edge, far_inner, background = lax.optimization_barrier((far_edge, far_inner, background))
    mid_lhs, rim_lhs, mean = cell_parts(PLON * lon_size, pos, stencil, frac, background)
    far_edge = swap(far_edge, half)
    far_inner, got, mid_lhs, rim_lhs, mean = lax.optimization_barrier((far_inner, got, mid_lhs, rim_lhs, mean))
    far_inner = swap(far_inner, half)

    left, right, edge, total, side = edge_transforms(got, far_edge)
    up = [(i, (i + 1) % lon_size) for i in range(lon_size)]
    down = [(j, i) for i, j in up]
    before = lax.ppermute(right, "lon", up)
    after = lax.ppermute(left, "lon", down)
    inner, *rows = inner_transforms(total, side, far_inner, left, right)
    rows = [rows[r].at[0].set(before[r]).at[PLON + 1].set(after[r]) for r in range(PLAT)]
    north = [(i, i + 1) for i in range(lat_size - 1)]
    south = [(j, i) for i, j in north]
    above = lax.ppermute(rows[PLAT - 1], "lat", north)
    below = lax.ppermute(rows[0], "lat", south)
    partial = mix(mid_kernel, [before, after, edge, inner], mid_lhs, mean, F32)
    return mix(rim_kernel, [above, below], rim_lhs, partial, BF16).reshape(background.shape)


def solution(mesh):
    return jax.shard_map(
        on_device,
        mesh=mesh,
        in_specs=(
            P(("lat", "lon"), None, None),
            P(("lat", "lon"), None),
            P(("lat", "lon"), None),
            P(("lat", "lon"), None),
            P(("lat", "lon"), None),
            P(("lat", "lon"), None),
            P(("lat", "lon")),
            P(("lat", "lon"), None),
            P("lat", "lon", None),
            P(None, "lat", "lon"),
            P(None, "lat", "lon"),
        ),
        out_specs=P("lat", "lon", None),
        check_vma=False,
    )
```

```python
import functools

import jax
import jax.numpy as jnp
from jax import lax
from jax.experimental import pallas as pl
from jax.experimental.pallas import tpu as pltpu
from jax.sharding import PartitionSpec as P

CAP = 4
PLAT = 2
PLON = 4
POINTS = PLAT * PLON
ITERS = 6
HALF = 128
MEMBERS = 2 * HALF
TILE = 16
BLOCK = CAP * MEMBERS + TILE
PACKED = MEMBERS + TILE
F32 = jnp.float32
BF16 = jnp.bfloat16
MIB = 1024 * 1024

SMEM_SPEC = pl.BlockSpec(memory_space=pltpu.SMEM)
VMEM_SPEC = pl.BlockSpec(memory_space=pltpu.VMEM)
ANY_SPEC = pl.BlockSpec(memory_space=pl.ANY)


def params(mebibytes):
    return pltpu.CompilerParams(vmem_limit_bytes=mebibytes * MIB)


def dot_nn(a, b):
    return lax.dot_general(a, b, (((1,), (0,)), ((), ())), preferred_element_type=F32)


def dot_nt(a, b):
    return lax.dot_general(a, b, (((1,), (1,)), ((), ())), preferred_element_type=F32)


def iota(shape, dim):
    return lax.broadcasted_iota(jnp.int32, shape, dim)


def gram_kernel(first, count, lon_size, me_ref, *refs):
    owner_hbm, len_hbm, points_hbm, num_hbm, weight_hbm, innov_hbm, taper_hbm, pert_ref = refs[:8]
    outs = refs[8:8 + count]
    (owner_ref, len_ref, points_ref, num_ref, weight_ref, innov_ref, taper_ref,
     source, filled, rows, w32, i32, t32, built, small_sem, in_sem, out_sem) = refs[8 + count:]
    held, nobs, _ = pert_ref.shape
    me = me_ref[0]
    loads = [
        pltpu.make_async_copy(a, b, small_sem.at[n])
        for n, (a, b) in enumerate((
            (owner_hbm, owner_ref), (len_hbm, len_ref), (points_hbm, points_ref), (num_hbm, num_ref),
            (weight_hbm, weight_ref), (innov_hbm, innov_ref), (taper_hbm, taper_ref)))]
    for load in loads:
        load.start()

    @pl.loop(0, lon_size)
    def _(k):
        filled[k] = 0

    @pl.loop(0, count * CAP)
    def _(s):
        source[first * CAP + s] = 0

    loads[0].wait()

    @pl.loop(0, held)
    def _(b):
        k = owner_ref[0, b] ^ me
        n = filled[k]
        source[k * CAP + n] = b
        filled[k] = n + 1

    def fetch(step, j):
        b = source[(first + step) * CAP + j]
        return pltpu.make_async_copy(pert_ref.at[b], rows.at[step, j], in_sem.at[step, j])

    @pl.loop(0, count)
    def _(step):
        for j in range(CAP):
            fetch(step, j).start()

    for load in loads[1:]:
        load.wait()
    w32[...] = weight_ref[...].astype(F32)
    i32[...] = innov_ref[...].astype(F32)
    t32[...] = jnp.concatenate(
        [taper_ref[...].astype(F32), jnp.zeros((8 - taper_ref.shape[0], held), F32)], axis=0)
    lane_obs = iota((1, nobs), 1)
    lane = iota((1, HALF), 1)
    lane_held = iota((1, held), 1)
    row_id = iota((HALF, HALF), 0)
    col_id = iota((HALF, HALF), 1)

    @pl.loop(0, count)
    def _(step):
        k = first + step
        for j in range(CAP):
            fetch(step, j).wait()
        lo, hi, dg, cf = [], [], [], []
        for j in range(CAP):
            b = source[k * CAP + j]
            present = j < filled[k]
            live = jnp.where(present, len_ref[0, b], 0)
            keep = jnp.where(lane_obs < live, w32[pl.ds(b, 1), :], 0.0)
            pulled = (keep * i32[pl.ds(b, 1), :]).astype(BF16)
            x = rows[step, j]
            scaled = x.T * keep.astype(BF16)
            lhs = jnp.concatenate([scaled, jnp.broadcast_to(pulled, (TILE, nobs))], axis=0)
            gram = dot_nn(lhs, x)
            a11 = gram[0:HALF, 0:HALF]
            a22 = gram[HALF:MEMBERS, HALF:MEMBERS]
            built[step, pl.ds(j * MEMBERS, HALF), :] = jnp.where(row_id <= col_id, a11, a22).astype(BF16)
            built[step, pl.ds(j * MEMBERS + HALF, HALF), :] = gram[0:HALF, HALF:MEMBERS].astype(BF16)
            lo.append(gram[MEMBERS:MEMBERS + 1, 0:HALF])
            hi.append(gram[MEMBERS:MEMBERS + 1, HALF:MEMBERS])
            dg.append(jnp.sum(jnp.where(row_id == col_id, a22, 0.0), axis=0, keepdims=True))
            limit = jnp.where(present, num_ref[b], 0)
            coef = jnp.zeros((1, HALF), F32)
            for q in range(3):
                taper = jnp.sum(jnp.where(lane_held == b, t32[q:q + 1, :], 0.0), axis=1, keepdims=True)
                hit = (lane == points_ref[q, b]) & (q < limit)
                coef = coef + jnp.where(hit, taper, 0.0)
            cf.append(coef)
        built[step, pl.ds(CAP * MEMBERS, TILE), :] = jnp.concatenate(lo + hi + dg + cf, axis=0).astype(BF16)
        for i in range(count):
            @pl.when(step == i)
            def _():
                pltpu.make_async_copy(built.at[i], outs[i], out_sem.at[i]).start()

    for i in range(count):
        pltpu.make_async_copy(built.at[i], outs[i], out_sem.at[i]).wait()


def batch_blocks(room, first, count, lon_size, me, owner, length, points, num, weight, innov, taper, pert):
    held, nobs, members = pert.shape
    return pl.pallas_call(
        functools.partial(gram_kernel, first, count, lon_size),
        out_shape=[jax.ShapeDtypeStruct((BLOCK, HALF), BF16)] * count,
        in_specs=[SMEM_SPEC] + [ANY_SPEC] * 8,
        out_specs=[ANY_SPEC] * count,
        scratch_shapes=[
            pltpu.SMEM(owner.shape, jnp.int32),
            pltpu.SMEM(length.shape, jnp.int32),
            pltpu.SMEM(points.shape, jnp.int32),
            pltpu.SMEM(num.shape, jnp.int32),
            pltpu.VMEM(weight.shape, BF16),
            pltpu.VMEM(innov.shape, BF16),
            pltpu.VMEM(taper.shape, BF16),
            pltpu.SMEM((lon_size * CAP,), jnp.int32),
            pltpu.SMEM((lon_size,), jnp.int32),
            pltpu.VMEM((count, CAP, nobs, members), BF16),
            pltpu.VMEM((held, nobs), F32),
            pltpu.VMEM((held, nobs), F32),
            pltpu.VMEM((8, held), F32),
            pltpu.VMEM((count, BLOCK, HALF), BF16),
            pltpu.SemaphoreType.DMA((7,)),
            pltpu.SemaphoreType.DMA((count, CAP)),
            pltpu.SemaphoreType.DMA((count,)),
        ],
        compiler_params=params(room),
        cost_estimate=pl.CostEstimate(
            flops=count * CAP * 2 * nobs * members * members,
            bytes_accessed=count * CAP * nobs * members * 2, transcendentals=0),
    )(me, owner, length, points, num, weight, innov, taper, pert)


EDGE = [r * PLON + c for r in range(PLAT) for c in (0, PLON - 1)]
INNER = [r * PLON + c for r in range(PLAT) for c in range(1, PLON - 1)]


def unpack(triangle, corner, diagonal):
    row_id = iota((HALF, HALF), 0)
    col_id = iota((HALF, HALF), 1)
    flipped = triangle.T
    a11 = jnp.where(row_id <= col_id, triangle, flipped)
    a22 = jnp.where(row_id > col_id, triangle, jnp.where(row_id == col_id, diagonal, flipped))
    return jnp.concatenate(
        [jnp.concatenate([a11, corner], axis=1), jnp.concatenate([corner.T, a22], axis=1)], axis=0)


def pack(matrix):
    row_id = iota((HALF, HALF), 0)
    col_id = iota((HALF, HALF), 1)
    a22 = matrix[HALF:MEMBERS, HALF:MEMBERS]
    triangle = jnp.where(row_id <= col_id, matrix[0:HALF, 0:HALF], a22)
    diagonal = jnp.sum(jnp.where(row_id == col_id, a22, 0.0), axis=0, keepdims=True)
    return triangle, matrix[0:HALF, HALF:MEMBERS], diagonal


def sum_by_point(blocks, acc, side):
    slots = len(blocks) * CAP
    extras = [blk[pl.ds(CAP * MEMBERS, TILE), :].astype(F32) for blk in blocks]
    low, high, diag, coef = [
        jnp.concatenate([e[CAP * q:CAP * (q + 1)] for e in extras], axis=0).astype(BF16) for q in range(4)]
    pick = (iota((POINTS, HALF), 0) == iota((POINTS, HALF), 1)).astype(BF16)
    by_point = dot_nt(pick, coef).astype(BF16)
    for q, part in enumerate((diag, low, high)):
        side[q] = dot_nn(by_point, part)
    spread = (iota((POINTS * TILE, HALF), 0) // TILE == iota((POINTS * TILE, HALF), 1)).astype(BF16)
    tall = dot_nt(spread, coef).astype(BF16)
    wide = (iota((slots, slots * TILE), 1) // TILE == iota((slots, slots * TILE), 0)).astype(BF16)
    mixing = dot_nn(tall, wide)
    shape = (POINTS * TILE, slots * TILE)
    mixing = jnp.where(iota(shape, 0) % TILE == iota(shape, 1) % TILE, mixing, 0.0).astype(BF16)
    for g in range(0, MEMBERS // TILE, 2):
        pair = []
        for h in (g, g + 1):
            pair.append(jnp.concatenate(
                [blk[pl.ds(j * MEMBERS + h * TILE, TILE), :] for blk in blocks for j in range(CAP)], axis=0))
        summed = dot_nn(mixing, jnp.concatenate(pair, axis=1))
        for p in range(POINTS):
            for h in (0, 1):
                acc[p, pl.ds((g + h) * TILE, TILE), :] = summed[p * TILE:(p + 1) * TILE, h * HALF:(h + 1) * HALF]


def relay_kernel(count, *refs):
    blocks = refs[:count]
    edge_ref, inner_ref, acc, side = refs[count:]
    sum_by_point(blocks, acc, side)
    for ref, listed in ((edge_ref, EDGE), (inner_ref, INNER)):
        rows = []
        for i, p in enumerate(listed):
            ref[pl.ds(i * MEMBERS, MEMBERS), :] = acc[p].astype(BF16)
            rows += [side[q, pl.ds(p, 1), :] for q in range(3)]
        rows.append(jnp.zeros((TILE - len(rows), HALF), F32))
        ref[pl.ds(len(listed) * MEMBERS, TILE), :] = jnp.concatenate(rows, axis=0).astype(BF16)


def relay_sums(blocks):
    return pl.pallas_call(
        functools.partial(relay_kernel, len(blocks)),
        out_shape=[
            jax.ShapeDtypeStruct((len(EDGE) * MEMBERS + TILE, HALF), BF16),
            jax.ShapeDtypeStruct((len(INNER) * MEMBERS + TILE, HALF), BF16),
        ],
        in_specs=[VMEM_SPEC] * len(blocks),
        out_specs=[VMEM_SPEC] * 2,
        scratch_shapes=[
            pltpu.VMEM((POINTS, MEMBERS, HALF), F32),
            pltpu.VMEM((3, POINTS, HALF), F32),
        ],
        compiler_params=params(6 + len(blocks)),
        cost_estimate=pl.CostEstimate(
            flops=len(blocks) * CAP * POINTS * TILE * MEMBERS * HALF,
            bytes_accessed=len(blocks) * BLOCK * HALF * 4, transcendentals=0),
    )(*blocks)


def transform_points(listed, total_of, side_of, far_ref, scratch, full_ref, packed_out):
    w32, z32, wb, gb, zb = scratch
    eye = (iota((MEMBERS, MEMBERS), 0) == iota((MEMBERS, MEMBERS), 1)).astype(F32)
    scales, shifts = [], []
    points = range(len(listed))
    extra = far_ref[pl.ds(len(listed) * MEMBERS, TILE), :].astype(F32)
    for i in points:
        p = listed[i]
        packed = total_of(p) + far_ref[pl.ds(i * MEMBERS, MEMBERS), :].astype(F32)
        diagonal, low, high = [side_of(p)[q] + extra[3 * i + q:3 * i + q + 1] for q in range(3)]
        shifts.append(jnp.concatenate([low, high], axis=1))
        system = unpack(packed[0:HALF], packed[HALF:MEMBERS], diagonal) + (MEMBERS - 1) * eye
        square = jnp.sum(jnp.sum(system * system, axis=0, keepdims=True), axis=1, keepdims=True)
        inv = lax.rsqrt(square)
        inv = inv * (1.5 - 0.5 * square * inv * inv)
        scales.append(inv)
        iterate = system * inv
        root = 1.5 * eye - 0.5 * iterate
        w32[i] = iterate
        wb[i] = iterate.astype(BF16)
        z32[i] = root
        zb[i] = root.astype(BF16)

    def advance():
        for i in points:
            gb[i] = (0.25 * dot_nn(wb[i], wb[i]) - 1.5 * w32[i]).astype(BF16)
        for i in points:
            value = 2.25 * w32[i] + dot_nn(wb[i], gb[i])
            w32[i] = value
            wb[i] = value.astype(BF16)

    advance()

    for sweep in range(ITERS - 2):
        for i in points:
            value = 1.5 * z32[i] - 0.5 * dot_nn(wb[i], zb[i])
            z32[i] = value
            zb[i] = value.astype(BF16)
        advance()

    for i in points:
        z32[i] = 1.5 * z32[i] - 0.5 * dot_nn(wb[i], zb[i])
    for i in points:
        root = z32[i]
        inner = jnp.sum(root * shifts[i], axis=1, keepdims=True)
        mean_weight = jnp.sum(root * inner, axis=0, keepdims=True) * scales[i]
        result = root * jnp.sqrt((MEMBERS - 1) * scales[i])
        column = jnp.broadcast_to(mean_weight, (HALF, MEMBERS)).T
        full_ref[i] = (result + jnp.concatenate([column, column], axis=1)).astype(BF16)
        triangle, corner, diagonal = pack(result)
        extra = jnp.concatenate(
            [diagonal, mean_weight[:, 0:HALF], mean_weight[:, HALF:MEMBERS], jnp.zeros((TILE - 3, HALF), F32)],
            axis=0)
        for ref, where in packed_out(listed[i]):
            ref[where, pl.ds(0, HALF), :] = triangle.astype(BF16)
            ref[where, pl.ds(HALF, HALF), :] = corner.astype(BF16)
            ref[where, pl.ds(MEMBERS, TILE), :] = extra.astype(BF16)


def edge_kernel(count, *refs):
    blocks = refs[:count]
    far_ref, left_ref, right_ref = refs[count:count + 3]
    rows = refs[count + 3:count + 3 + PLAT]
    full_ref, total_ref, side_ref, w32, z32, wb, gb, zb, acc = refs[count + 3 + PLAT:]
    sum_by_point(blocks, acc, side_ref)
    for i, p in enumerate(INNER):
        total_ref[i] = acc[p]
    transform_points(
        EDGE,
        lambda p: acc[p],
        lambda p: [side_ref[q, pl.ds(p, 1), :] for q in range(3)],
        far_ref, (w32, z32, wb, gb, zb), full_ref,
        lambda p: [
            (left_ref if p % PLON == 0 else right_ref, p // PLON), (rows[p // PLON], 0 if p % PLON == 0 else 1)])


def inner_kernel(total_in, side_in, far_ref, full_ref, *refs):
    rows, scratch = refs[:PLAT], refs[PLAT:]
    transform_points(
        INNER,
        lambda p: total_in[INNER.index(p)],
        lambda p: [side_in[q, pl.ds(p, 1), :] for q in range(3)],
        far_ref, scratch, full_ref,
        lambda p: [(rows[p // PLON], p % PLON)])


def newton_scratch(count):
    shape = (count, MEMBERS, MEMBERS)
    return [pltpu.VMEM(shape, F32)] * 2 + [pltpu.VMEM(shape, BF16)] * 3


def edge_transforms(blocks, far):
    columns = jax.ShapeDtypeStruct((PLAT, PACKED, HALF), BF16)
    return pl.pallas_call(
        functools.partial(edge_kernel, len(blocks)),
        out_shape=[
            columns, columns,
            *[jax.ShapeDtypeStruct((2, PACKED, HALF), BF16)] * PLAT,
            jax.ShapeDtypeStruct((len(EDGE), MEMBERS, MEMBERS), BF16),
            jax.ShapeDtypeStruct((len(INNER), MEMBERS, HALF), F32),
            jax.ShapeDtypeStruct((3, POINTS, HALF), F32),
        ],
        in_specs=[VMEM_SPEC] * (len(blocks) + 1),
        out_specs=[VMEM_SPEC] * (5 + PLAT),
        scratch_shapes=newton_scratch(len(EDGE)) + [pltpu.VMEM((POINTS, MEMBERS, HALF), F32)],
        compiler_params=params(12 + len(blocks)),
        cost_estimate=pl.CostEstimate(
            flops=len(EDGE) * 15 * 2 * MEMBERS ** 3, bytes_accessed=8 * MEMBERS * HALF * 6, transcendentals=0),
    )(*blocks, far)


def inner_transforms(total, side, far):
    count = total.shape[0]
    row = jax.ShapeDtypeStruct((PLON, PACKED, HALF), BF16)
    return pl.pallas_call(
        inner_kernel,
        out_shape=[jax.ShapeDtypeStruct((count, MEMBERS, MEMBERS), BF16)] + [row] * PLAT,
        in_specs=[VMEM_SPEC] * 3,
        out_specs=[VMEM_SPEC] * (1 + PLAT),
        scratch_shapes=newton_scratch(count),
        compiler_params=params(12),
        cost_estimate=pl.CostEstimate(
            flops=count * 15 * 2 * MEMBERS ** 3, bytes_accessed=count * MEMBERS * HALF * 6, transcendentals=0),
    )(total, side, far)


WIDE = PLON + 2
WINDOW = (PLAT + 2) * WIDE
MID = list(range(WIDE, WINDOW - WIDE))
RIM = list(range(WIDE)) + list(range(WINDOW - WIDE, WINDOW))


def cell_kernel(point_cols, pos_ref, stencil_ref, frac_ref, field_ref, kept_in, mid_ref, rim_ref, mean_ref,
                kept_out):
    width = stencil_ref.shape[2]
    lat_pos, lon_pos = pos_ref[0], pos_ref[1]
    i = pl.program_id(0)

    @pl.when(i == 0)
    def _():
        kept_out[...] = kept_in[...]

    ids = iota((HALF, width), 0)
    field = field_ref[0].astype(F32)
    mean = jnp.mean(field, axis=1, keepdims=True)
    mean_ref[...] = jnp.broadcast_to(mean, mean_ref.shape)
    dev = (field - mean).astype(BF16).astype(F32)
    row_off = stencil_ref[0, pl.ds(i, 1), :] - (lat_pos * PLAT - 1)
    col_off = stencil_ref[1, pl.ds(i, 1), :] - (lon_pos * PLON - 1)
    col_off = jnp.where(col_off < 0, col_off + point_cols, col_off)
    col_off = jnp.where(col_off >= point_cols, col_off - point_cols, col_off)
    y = frac_ref[0, pl.ds(i, 1), :]
    x = frac_ref[1, pl.ds(i, 1), :]
    corner = row_off * WIDE + col_off
    weights = jnp.where(corner == ids, (1.0 - y) * (1.0 - x), 0.0)
    weights = weights + jnp.where(corner + WIDE == ids, y * (1.0 - x), 0.0)
    weights = weights + jnp.where(corner + 1 == ids, (1.0 - y) * x, 0.0)
    weights = weights + jnp.where(corner + WIDE + 1 == ids, y * x, 0.0)
    turned = weights.T
    for ref, listed in ((mid_ref, MID), (rim_ref, RIM)):
        for n, point in enumerate(listed):
            ref[:, n * MEMBERS:(n + 1) * MEMBERS] = (dev * turned[:, point:point + 1]).astype(BF16)


def cell_parts(point_cols, pos, stencil, frac, background, kept):
    rows, width, members = background.shape
    cells = rows * width
    return pl.pallas_call(
        functools.partial(cell_kernel, point_cols),
        grid=(rows,),
        out_shape=[
            jax.ShapeDtypeStruct((cells, len(MID) * members), BF16),
            jax.ShapeDtypeStruct((cells, len(RIM) * members), BF16),
            jax.ShapeDtypeStruct((cells, HALF), F32),
            jax.ShapeDtypeStruct(kept.shape, kept.dtype),
        ],
        in_specs=[
            SMEM_SPEC,
            pl.BlockSpec(stencil.shape, lambda i: (0, 0, 0)),
            pl.BlockSpec(frac.shape, lambda i: (0, 0, 0)),
            pl.BlockSpec((1, width, members), lambda i: (i, 0, 0)),
            pl.BlockSpec(kept.shape, lambda i: (0, 0)),
        ],
        out_specs=[
            pl.BlockSpec((width, len(MID) * members), lambda i: (i, 0)),
            pl.BlockSpec((width, len(RIM) * members), lambda i: (i, 0)),
            pl.BlockSpec((width, HALF), lambda i: (i, 0)),
            pl.BlockSpec(kept.shape, lambda i: (0, 0)),
        ],
        compiler_params=params(12),
        cost_estimate=pl.CostEstimate(
            flops=cells * members * WINDOW, bytes_accessed=cells * members * (2 * WINDOW + 4), transcendentals=0),
    )(pos, stencil, frac, background, kept)


def place_packed(matrices, slot, ref, i):
    extra = ref[i, pl.ds(MEMBERS, TILE), :].astype(F32)
    full = unpack(ref[i, pl.ds(0, HALF), :].astype(F32), ref[i, pl.ds(HALF, HALF), :].astype(F32), extra[0:1])
    row = jnp.concatenate([extra[1:2], extra[2:3]], axis=1)
    column = jnp.broadcast_to(row, (HALF, MEMBERS)).T
    full = full + jnp.concatenate([column, column], axis=1)
    matrices[pl.ds(slot * MEMBERS, MEMBERS), :] = full.astype(BF16)


def mid_kernel(before, after, edge, inner, lhs_ref, mean_ref, out_ref, matrices):
    for r in range(PLAT):
        place_packed(matrices, r * WIDE, before, r)
        place_packed(matrices, r * WIDE + PLON + 1, after, r)
        for c in range(PLON):
            p = r * PLON + c
            value = edge[EDGE.index(p)] if p in EDGE else inner[INNER.index(p)]
            matrices[pl.ds((r * WIDE + c + 1) * MEMBERS, MEMBERS), :] = value

    out_ref[...] = dot_nn(lhs_ref[...], matrices[...]) + mean_ref[:, 0:1]


def rim_kernel(above_edge, below_edge, above, below, lhs_ref, base_ref, out_ref, matrices):
    for row, edge, rest in ((0, above_edge, above), (1, below_edge, below)):
        for i, c in enumerate((0, PLON - 1)):
            place_packed(matrices, row * WIDE + c + 1, edge, i)
        for i, c in enumerate([-1] + list(range(1, PLON - 1)) + [PLON]):
            place_packed(matrices, row * WIDE + c + 1, rest, i)

    out_ref[...] = (dot_nn(lhs_ref[...], matrices[...]) + base_ref[...]).astype(BF16)


def mix(kernel, transforms, lhs, base, dtype):
    cells, depth = lhs.shape
    return pl.pallas_call(
        kernel,
        out_shape=jax.ShapeDtypeStruct((cells, MEMBERS), dtype),
        in_specs=[VMEM_SPEC] * (len(transforms) + 2),
        out_specs=VMEM_SPEC,
        scratch_shapes=[pltpu.VMEM((depth, MEMBERS), BF16)],
        compiler_params=params(20),
        cost_estimate=pl.CostEstimate(
            flops=2 * cells * depth * MEMBERS, bytes_accessed=cells * depth * 2, transcendentals=0),
    )(*transforms, lhs, base)


def on_device(obs_pert, obs_weight, innovation, batch_len, batch_owner, batch_points, batch_count,
              batch_taper, background, stencil, frac):
    lon_size, lat_size = lax.axis_size("lon"), lax.axis_size("lat")
    lat_pos, lon_pos = lax.axis_index("lat"), lax.axis_index("lon")
    me = lon_pos.astype(jnp.int32).reshape(1)
    pos = jnp.stack([lat_pos, lon_pos]).astype(jnp.int32)
    fixed = (me, batch_owner.T, batch_len, batch_points.T, batch_count, obs_weight, innovation, batch_taper.T,
             obs_pert)
    half = lon_size // 2

    def swap(value, offset):
        return lax.ppermute(value, "lon", [(i, i ^ offset) for i in range(lon_size)])

    far = batch_blocks(57, half + 1, half - 1, lon_size, *fixed)
    relayed = [swap(far[i - 1], i) for i in range(1, half)]
    *near, own_far = batch_blocks(57, 1, half, lon_size, *fixed)
    got = [swap(near[i - 1], i) for i in range(1, half)]
    obs_pert, near, own_far = lax.optimization_barrier((obs_pert, near, own_far))
    own_near, = batch_blocks(57, 0, 1, lon_size, *fixed[:-1], obs_pert)
    relayed, own_near = lax.optimization_barrier((relayed, own_near))
    far_edge, far_inner = relay_sums([own_far] + relayed)
    far_edge, far_inner, background = lax.optimization_barrier((far_edge, far_inner, background))
    mid_lhs, rim_lhs, mean, own_near = cell_parts(PLON * lon_size, pos, stencil, frac, background, own_near)
    got = [own_near] + got
    far_edge = swap(far_edge, half)
    far_inner, got, mid_lhs, rim_lhs, mean = lax.optimization_barrier((far_inner, got, mid_lhs, rim_lhs, mean))
    far_inner = swap(far_inner, half)

    left, right, *edge_rows, edge, total, side = edge_transforms(got, far_edge)
    up = [(i, (i + 1) % lon_size) for i in range(lon_size)]
    down = [(j, i) for i, j in up]
    north = [(i, i + 1) for i in range(lat_size - 1)]
    south = [(j, i) for i, j in north]
    before = lax.ppermute(right, "lon", up)
    after = lax.ppermute(left, "lon", down)
    above_edge = lax.ppermute(edge_rows[PLAT - 1], "lat", north)
    below_edge = lax.ppermute(edge_rows[0], "lat", south)
    far_inner, above_edge, below_edge = lax.optimization_barrier((far_inner, above_edge, below_edge))
    inner, *rows = inner_transforms(total, side, far_inner)
    rows = [rows[r].at[0].set(before[r]).at[PLON - 1].set(after[r]) for r in range(PLAT)]
    above = lax.ppermute(rows[PLAT - 1], "lat", north)
    below = lax.ppermute(rows[0], "lat", south)
    partial = mix(mid_kernel, [before, after, edge, inner], mid_lhs, mean, F32)
    return mix(rim_kernel, [above_edge, below_edge, above, below], rim_lhs, partial, BF16).reshape(background.shape)


def solution(mesh):
    return jax.shard_map(
        on_device,
        mesh=mesh,
        in_specs=(
            P(("lat", "lon"), None, None),
            P(("lat", "lon"), None),
            P(("lat", "lon"), None),
            P(("lat", "lon"), None),
            P(("lat", "lon"), None),
            P(("lat", "lon"), None),
            P(("lat", "lon")),
            P(("lat", "lon"), None),
            P("lat", "lon", None),
            P(None, "lat", "lon"),
            P(None, "lat", "lon"),
        ),
        out_specs=P("lat", "lon", None),
        check_vma=False,
    )
```

```python
import functools

import jax
import jax.numpy as jnp
from jax import lax
from jax.experimental import pallas as pl
from jax.experimental.pallas import tpu as pltpu
from jax.sharding import PartitionSpec as P

CAP = 4
PLAT = 2
PLON = 4
POINTS = PLAT * PLON
ITERS = 6
HALF = 128
MEMBERS = 2 * HALF
TILE = 16
BLOCK = CAP * MEMBERS + TILE
PACKED = MEMBERS + TILE
F32 = jnp.float32
BF16 = jnp.bfloat16
MIB = 1024 * 1024

SMEM_SPEC = pl.BlockSpec(memory_space=pltpu.SMEM)
VMEM_SPEC = pl.BlockSpec(memory_space=pltpu.VMEM)
ANY_SPEC = pl.BlockSpec(memory_space=pl.ANY)


def params(mebibytes):
    return pltpu.CompilerParams(vmem_limit_bytes=mebibytes * MIB)


def dot_nn(a, b):
    return lax.dot_general(a, b, (((1,), (0,)), ((), ())), preferred_element_type=F32)


def dot_nt(a, b):
    return lax.dot_general(a, b, (((1,), (1,)), ((), ())), preferred_element_type=F32)


def iota(shape, dim):
    return lax.broadcasted_iota(jnp.int32, shape, dim)


def gram_kernel(first, count, lon_size, me_ref, *refs):
    owner_hbm, len_hbm, points_hbm, num_hbm, weight_hbm, innov_hbm, taper_hbm, pert_ref = refs[:8]
    outs = refs[8:8 + count]
    (owner_ref, len_ref, points_ref, num_ref, weight_ref, innov_ref, taper_ref,
     source, filled, rows, w32, i32, t32, built, small_sem, in_sem, out_sem) = refs[8 + count:]
    held, nobs, _ = pert_ref.shape
    me = me_ref[0]
    loads = [
        pltpu.make_async_copy(a, b, small_sem.at[n])
        for n, (a, b) in enumerate((
            (owner_hbm, owner_ref), (len_hbm, len_ref), (points_hbm, points_ref), (num_hbm, num_ref),
            (weight_hbm, weight_ref), (innov_hbm, innov_ref), (taper_hbm, taper_ref)))]
    for load in loads:
        load.start()

    @pl.loop(0, lon_size)
    def _(k):
        filled[k] = 0

    @pl.loop(0, count * CAP)
    def _(s):
        source[first * CAP + s] = 0

    loads[0].wait()

    @pl.loop(0, held)
    def _(b):
        k = owner_ref[0, b] ^ me
        n = filled[k]
        source[k * CAP + n] = b
        filled[k] = n + 1

    def fetch(step, j):
        b = source[(first + step) * CAP + j]
        return pltpu.make_async_copy(pert_ref.at[b], rows.at[step, j], in_sem.at[step, j])

    @pl.loop(0, count)
    def _(step):
        for j in range(CAP):
            fetch(step, j).start()

    for load in loads[1:]:
        load.wait()
    w32[...] = weight_ref[...].astype(F32)
    i32[...] = innov_ref[...].astype(F32)
    t32[...] = jnp.concatenate(
        [taper_ref[...].astype(F32), jnp.zeros((8 - taper_ref.shape[0], held), F32)], axis=0)
    lane_obs = iota((1, nobs), 1)
    lane = iota((1, HALF), 1)
    lane_held = iota((1, held), 1)
    row_id = iota((HALF, HALF), 0)
    col_id = iota((HALF, HALF), 1)

    @pl.loop(0, count)
    def _(step):
        k = first + step
        for j in range(CAP):
            fetch(step, j).wait()
        lo, hi, dg, cf = [], [], [], []
        for j in range(CAP):
            b = source[k * CAP + j]
            present = j < filled[k]
            live = jnp.where(present, len_ref[0, b], 0)
            keep = jnp.where(lane_obs < live, w32[pl.ds(b, 1), :], 0.0)
            pulled = (keep * i32[pl.ds(b, 1), :]).astype(BF16)
            x = rows[step, j]
            scaled = x.T * keep.astype(BF16)
            lhs = jnp.concatenate([scaled, jnp.broadcast_to(pulled, (TILE, nobs))], axis=0)
            gram = dot_nn(lhs, x)
            a11 = gram[0:HALF, 0:HALF]
            a22 = gram[HALF:MEMBERS, HALF:MEMBERS]
            built[step, pl.ds(j * MEMBERS, HALF), :] = jnp.where(row_id <= col_id, a11, a22).astype(BF16)
            built[step, pl.ds(j * MEMBERS + HALF, HALF), :] = gram[0:HALF, HALF:MEMBERS].astype(BF16)
            lo.append(gram[MEMBERS:MEMBERS + 1, 0:HALF])
            hi.append(gram[MEMBERS:MEMBERS + 1, HALF:MEMBERS])
            dg.append(jnp.sum(jnp.where(row_id == col_id, a22, 0.0), axis=0, keepdims=True))
            limit = jnp.where(present, num_ref[b], 0)
            coef = jnp.zeros((1, HALF), F32)
            for q in range(3):
                taper = jnp.sum(jnp.where(lane_held == b, t32[q:q + 1, :], 0.0), axis=1, keepdims=True)
                hit = (lane == points_ref[q, b]) & (q < limit)
                coef = coef + jnp.where(hit, taper, 0.0)
            cf.append(coef)
        built[step, pl.ds(CAP * MEMBERS, TILE), :] = jnp.concatenate(lo + hi + dg + cf, axis=0).astype(BF16)
        for i in range(count):
            @pl.when(step == i)
            def _():
                pltpu.make_async_copy(built.at[i], outs[i], out_sem.at[i]).start()

    for i in range(count):
        pltpu.make_async_copy(built.at[i], outs[i], out_sem.at[i]).wait()


def batch_blocks(room, first, count, lon_size, me, owner, length, points, num, weight, innov, taper, pert):
    held, nobs, members = pert.shape
    return pl.pallas_call(
        functools.partial(gram_kernel, first, count, lon_size),
        out_shape=[jax.ShapeDtypeStruct((BLOCK, HALF), BF16)] * count,
        in_specs=[SMEM_SPEC] + [ANY_SPEC] * 8,
        out_specs=[ANY_SPEC] * count,
        scratch_shapes=[
            pltpu.SMEM(owner.shape, jnp.int32),
            pltpu.SMEM(length.shape, jnp.int32),
            pltpu.SMEM(points.shape, jnp.int32),
            pltpu.SMEM(num.shape, jnp.int32),
            pltpu.VMEM(weight.shape, BF16),
            pltpu.VMEM(innov.shape, BF16),
            pltpu.VMEM(taper.shape, BF16),
            pltpu.SMEM((lon_size * CAP,), jnp.int32),
            pltpu.SMEM((lon_size,), jnp.int32),
            pltpu.VMEM((count, CAP, nobs, members), BF16),
            pltpu.VMEM((held, nobs), F32),
            pltpu.VMEM((held, nobs), F32),
            pltpu.VMEM((8, held), F32),
            pltpu.VMEM((count, BLOCK, HALF), BF16),
            pltpu.SemaphoreType.DMA((7,)),
            pltpu.SemaphoreType.DMA((count, CAP)),
            pltpu.SemaphoreType.DMA((count,)),
        ],
        compiler_params=params(room),
        cost_estimate=pl.CostEstimate(
            flops=count * CAP * 2 * nobs * members * members,
            bytes_accessed=count * CAP * nobs * members * 2, transcendentals=0),
    )(me, owner, length, points, num, weight, innov, taper, pert)


EDGE = [r * PLON + c for r in range(PLAT) for c in (0, PLON - 1)]
INNER = [r * PLON + c for r in range(PLAT) for c in range(1, PLON - 1)]


def unpack(triangle, corner, diagonal):
    row_id = iota((HALF, HALF), 0)
    col_id = iota((HALF, HALF), 1)
    flipped = triangle.T
    a11 = jnp.where(row_id <= col_id, triangle, flipped)
    a22 = jnp.where(row_id > col_id, triangle, jnp.where(row_id == col_id, diagonal, flipped))
    return jnp.concatenate(
        [jnp.concatenate([a11, corner], axis=1), jnp.concatenate([corner.T, a22], axis=1)], axis=0)


def pack(matrix):
    row_id = iota((HALF, HALF), 0)
    col_id = iota((HALF, HALF), 1)
    a22 = matrix[HALF:MEMBERS, HALF:MEMBERS]
    triangle = jnp.where(row_id <= col_id, matrix[0:HALF, 0:HALF], a22)
    diagonal = jnp.sum(jnp.where(row_id == col_id, a22, 0.0), axis=0, keepdims=True)
    return triangle, matrix[0:HALF, HALF:MEMBERS], diagonal


def sum_by_point(blocks, acc, side):
    slots = len(blocks) * CAP
    extras = [blk[pl.ds(CAP * MEMBERS, TILE), :].astype(F32) for blk in blocks]
    low, high, diag, coef = [
        jnp.concatenate([e[CAP * q:CAP * (q + 1)] for e in extras], axis=0).astype(BF16) for q in range(4)]
    pick = (iota((POINTS, HALF), 0) == iota((POINTS, HALF), 1)).astype(BF16)
    by_point = dot_nt(pick, coef).astype(BF16)
    for q, part in enumerate((diag, low, high)):
        side[q] = dot_nn(by_point, part)
    spread = (iota((POINTS * TILE, HALF), 0) // TILE == iota((POINTS * TILE, HALF), 1)).astype(BF16)
    tall = dot_nt(spread, coef).astype(BF16)
    wide = (iota((slots, slots * TILE), 1) // TILE == iota((slots, slots * TILE), 0)).astype(BF16)
    mixing = dot_nn(tall, wide)
    shape = (POINTS * TILE, slots * TILE)
    mixing = jnp.where(iota(shape, 0) % TILE == iota(shape, 1) % TILE, mixing, 0.0).astype(BF16)
    for g in range(0, MEMBERS // TILE, 2):
        pair = []
        for h in (g, g + 1):
            pair.append(jnp.concatenate(
                [blk[pl.ds(j * MEMBERS + h * TILE, TILE), :] for blk in blocks for j in range(CAP)], axis=0))
        summed = dot_nn(mixing, jnp.concatenate(pair, axis=1))
        for p in range(POINTS):
            for h in (0, 1):
                acc[p, pl.ds((g + h) * TILE, TILE), :] = summed[p * TILE:(p + 1) * TILE, h * HALF:(h + 1) * HALF]


def relay_kernel(count, *refs):
    blocks = refs[:count]
    edge_ref, inner_ref, acc, side = refs[count:]
    sum_by_point(blocks, acc, side)
    for ref, listed in ((edge_ref, EDGE), (inner_ref, INNER)):
        rows = []
        for i, p in enumerate(listed):
            ref[pl.ds(i * MEMBERS, MEMBERS), :] = acc[p].astype(BF16)
            rows += [side[q, pl.ds(p, 1), :] for q in range(3)]
        rows.append(jnp.zeros((TILE - len(rows), HALF), F32))
        ref[pl.ds(len(listed) * MEMBERS, TILE), :] = jnp.concatenate(rows, axis=0).astype(BF16)


def relay_sums(blocks):
    return pl.pallas_call(
        functools.partial(relay_kernel, len(blocks)),
        out_shape=[
            jax.ShapeDtypeStruct((len(EDGE) * MEMBERS + TILE, HALF), BF16),
            jax.ShapeDtypeStruct((len(INNER) * MEMBERS + TILE, HALF), BF16),
        ],
        in_specs=[VMEM_SPEC] * len(blocks),
        out_specs=[VMEM_SPEC] * 2,
        scratch_shapes=[
            pltpu.VMEM((POINTS, MEMBERS, HALF), F32),
            pltpu.VMEM((3, POINTS, HALF), F32),
        ],
        compiler_params=params(6 + len(blocks)),
        cost_estimate=pl.CostEstimate(
            flops=len(blocks) * CAP * POINTS * TILE * MEMBERS * HALF,
            bytes_accessed=len(blocks) * BLOCK * HALF * 4, transcendentals=0),
    )(*blocks)


def transform_points(listed, total_of, side_of, far_ref, scratch, full_ref, packed_out):
    w32, z32, wb, gb, zb = scratch
    eye = (iota((MEMBERS, MEMBERS), 0) == iota((MEMBERS, MEMBERS), 1)).astype(F32)
    scales, shifts = [], []
    points = range(len(listed))
    extra = far_ref[pl.ds(len(listed) * MEMBERS, TILE), :].astype(F32)
    for i in points:
        p = listed[i]
        packed = total_of(p) + far_ref[pl.ds(i * MEMBERS, MEMBERS), :].astype(F32)
        diagonal, low, high = [side_of(p)[q] + extra[3 * i + q:3 * i + q + 1] for q in range(3)]
        shifts.append(jnp.concatenate([low, high], axis=1))
        system = unpack(packed[0:HALF], packed[HALF:MEMBERS], diagonal) + (MEMBERS - 1) * eye
        square = jnp.sum(jnp.sum(system * system, axis=0, keepdims=True), axis=1, keepdims=True)
        inv = lax.rsqrt(square)
        inv = inv * (1.5 - 0.5 * square * inv * inv)
        scales.append(inv)
        iterate = system * inv
        root = 1.5 * eye - 0.5 * iterate
        w32[i] = iterate
        wb[i] = iterate.astype(BF16)
        z32[i] = root
        zb[i] = root.astype(BF16)

    def advance():
        for i in points:
            gb[i] = (0.25 * dot_nn(wb[i], wb[i]) - 1.5 * w32[i]).astype(BF16)
        for i in points:
            value = 2.25 * w32[i] + dot_nn(wb[i], gb[i])
            w32[i] = value
            wb[i] = value.astype(BF16)

    advance()

    for sweep in range(ITERS - 2):
        for i in points:
            value = 1.5 * z32[i] - 0.5 * dot_nn(wb[i], zb[i])
            z32[i] = value
            zb[i] = value.astype(BF16)
        advance()

    for i in points:
        z32[i] = 1.5 * z32[i] - 0.5 * dot_nn(wb[i], zb[i])
    for i in points:
        root = z32[i]
        inner = jnp.sum(root * shifts[i], axis=1, keepdims=True)
        mean_weight = jnp.sum(root * inner, axis=0, keepdims=True) * scales[i]
        result = root * jnp.sqrt((MEMBERS - 1) * scales[i])
        column = jnp.broadcast_to(mean_weight, (HALF, MEMBERS)).T
        full_ref[i] = (result + jnp.concatenate([column, column], axis=1)).astype(BF16)
        triangle, corner, diagonal = pack(result)
        extra = jnp.concatenate(
            [diagonal, mean_weight[:, 0:HALF], mean_weight[:, HALF:MEMBERS], jnp.zeros((TILE - 3, HALF), F32)],
            axis=0)
        for ref, where in packed_out(listed[i]):
            ref[where, pl.ds(0, HALF), :] = triangle.astype(BF16)
            ref[where, pl.ds(HALF, HALF), :] = corner.astype(BF16)
            ref[where, pl.ds(MEMBERS, TILE), :] = extra.astype(BF16)


def sum_kernel(count, *refs):
    total_ref, side_ref = refs[count:]
    sum_by_point(refs[:count], total_ref, side_ref)


def near_sums(blocks):
    count = len(blocks)
    return pl.pallas_call(
        functools.partial(sum_kernel, count),
        out_shape=[
            jax.ShapeDtypeStruct((POINTS, MEMBERS, HALF), F32),
            jax.ShapeDtypeStruct((3, POINTS, HALF), F32),
        ],
        in_specs=[VMEM_SPEC] * count,
        out_specs=[VMEM_SPEC] * 2,
        compiler_params=params(6 + count),
        cost_estimate=pl.CostEstimate(
            flops=count * CAP * POINTS * TILE * MEMBERS * HALF, bytes_accessed=count * BLOCK * HALF * 8, transcendentals=0),
    )(*blocks)


def edge_kernel(total_in, side_in, far_ref, left_ref, right_ref, *refs):
    rows, (full_ref, *scratch) = refs[:PLAT], refs[PLAT:]
    transform_points(
        EDGE,
        lambda p: total_in[p],
        lambda p: [side_in[q, pl.ds(p, 1), :] for q in range(3)],
        far_ref, scratch, full_ref,
        lambda p: [
            (left_ref if p % PLON == 0 else right_ref, p // PLON), (rows[p // PLON], 0 if p % PLON == 0 else 1)])


def inner_kernel(total_in, side_in, far_ref, full_ref, *refs):
    rows, scratch = refs[:PLAT], refs[PLAT:]
    transform_points(
        INNER,
        lambda p: total_in[p],
        lambda p: [side_in[q, pl.ds(p, 1), :] for q in range(3)],
        far_ref, scratch, full_ref,
        lambda p: [(rows[p // PLON], p % PLON)])


def newton_scratch(count):
    shape = (count, MEMBERS, MEMBERS)
    return [pltpu.VMEM(shape, F32)] * 2 + [pltpu.VMEM(shape, BF16)] * 3


def edge_transforms(total, side, far):
    count = len(EDGE)
    columns = jax.ShapeDtypeStruct((PLAT, PACKED, HALF), BF16)
    row = jax.ShapeDtypeStruct((2, PACKED, HALF), BF16)
    return pl.pallas_call(
        edge_kernel,
        out_shape=[columns, columns] + [row] * PLAT + [jax.ShapeDtypeStruct((count, MEMBERS, MEMBERS), BF16)],
        in_specs=[VMEM_SPEC] * 3,
        out_specs=[VMEM_SPEC] * (3 + PLAT),
        scratch_shapes=newton_scratch(count),
        compiler_params=params(12),
        cost_estimate=pl.CostEstimate(
            flops=count * 15 * 2 * MEMBERS ** 3, bytes_accessed=count * MEMBERS * HALF * 6, transcendentals=0),
    )(total, side, far)


def inner_transforms(total, side, far):
    count = len(INNER)
    row = jax.ShapeDtypeStruct((PLON, PACKED, HALF), BF16)
    return pl.pallas_call(
        inner_kernel,
        out_shape=[jax.ShapeDtypeStruct((count, MEMBERS, MEMBERS), BF16)] + [row] * PLAT,
        in_specs=[VMEM_SPEC] * 3,
        out_specs=[VMEM_SPEC] * (1 + PLAT),
        scratch_shapes=newton_scratch(count),
        compiler_params=params(12),
        cost_estimate=pl.CostEstimate(
            flops=count * 15 * 2 * MEMBERS ** 3, bytes_accessed=count * MEMBERS * HALF * 6, transcendentals=0),
    )(total, side, far)


WIDE = PLON + 2
WINDOW = (PLAT + 2) * WIDE
MID = list(range(WIDE, WINDOW - WIDE))
RIM = list(range(WIDE)) + list(range(WINDOW - WIDE, WINDOW))


def cell_kernel(point_cols, pos_ref, stencil_ref, frac_ref, field_ref, kept_in, mid_ref, rim_ref, mean_ref,
                kept_out):
    width = stencil_ref.shape[2]
    lat_pos, lon_pos = pos_ref[0], pos_ref[1]
    i = pl.program_id(0)

    @pl.when(i == 0)
    def _():
        kept_out[...] = kept_in[...]

    ids = iota((HALF, width), 0)
    field = field_ref[0].astype(F32)
    mean = jnp.mean(field, axis=1, keepdims=True)
    mean_ref[...] = jnp.broadcast_to(mean, mean_ref.shape)
    dev = (field - mean).astype(BF16).astype(F32)
    row_off = stencil_ref[0, pl.ds(i, 1), :] - (lat_pos * PLAT - 1)
    col_off = stencil_ref[1, pl.ds(i, 1), :] - (lon_pos * PLON - 1)
    col_off = jnp.where(col_off < 0, col_off + point_cols, col_off)
    col_off = jnp.where(col_off >= point_cols, col_off - point_cols, col_off)
    y = frac_ref[0, pl.ds(i, 1), :]
    x = frac_ref[1, pl.ds(i, 1), :]
    corner = row_off * WIDE + col_off
    weights = jnp.where(corner == ids, (1.0 - y) * (1.0 - x), 0.0)
    weights = weights + jnp.where(corner + WIDE == ids, y * (1.0 - x), 0.0)
    weights = weights + jnp.where(corner + 1 == ids, (1.0 - y) * x, 0.0)
    weights = weights + jnp.where(corner + WIDE + 1 == ids, y * x, 0.0)
    turned = weights.T
    for ref, listed in ((mid_ref, MID), (rim_ref, RIM)):
        for n, point in enumerate(listed):
            ref[:, n * MEMBERS:(n + 1) * MEMBERS] = (dev * turned[:, point:point + 1]).astype(BF16)


def cell_parts(point_cols, pos, stencil, frac, background, kept):
    rows, width, members = background.shape
    cells = rows * width
    return pl.pallas_call(
        functools.partial(cell_kernel, point_cols),
        grid=(rows,),
        out_shape=[
            jax.ShapeDtypeStruct((cells, len(MID) * members), BF16),
            jax.ShapeDtypeStruct((cells, len(RIM) * members), BF16),
            jax.ShapeDtypeStruct((cells, HALF), F32),
            jax.ShapeDtypeStruct(kept.shape, kept.dtype),
        ],
        in_specs=[
            SMEM_SPEC,
            pl.BlockSpec(stencil.shape, lambda i: (0, 0, 0)),
            pl.BlockSpec(frac.shape, lambda i: (0, 0, 0)),
            pl.BlockSpec((1, width, members), lambda i: (i, 0, 0)),
            pl.BlockSpec(kept.shape, lambda i: (0, 0)),
        ],
        out_specs=[
            pl.BlockSpec((width, len(MID) * members), lambda i: (i, 0)),
            pl.BlockSpec((width, len(RIM) * members), lambda i: (i, 0)),
            pl.BlockSpec((width, HALF), lambda i: (i, 0)),
            pl.BlockSpec(kept.shape, lambda i: (0, 0)),
        ],
        compiler_params=params(12),
        cost_estimate=pl.CostEstimate(
            flops=cells * members * WINDOW, bytes_accessed=cells * members * (2 * WINDOW + 4), transcendentals=0),
    )(pos, stencil, frac, background, kept)


def place_packed(matrices, slot, ref, i):
    extra = ref[i, pl.ds(MEMBERS, TILE), :].astype(F32)
    full = unpack(ref[i, pl.ds(0, HALF), :].astype(F32), ref[i, pl.ds(HALF, HALF), :].astype(F32), extra[0:1])
    row = jnp.concatenate([extra[1:2], extra[2:3]], axis=1)
    column = jnp.broadcast_to(row, (HALF, MEMBERS)).T
    full = full + jnp.concatenate([column, column], axis=1)
    matrices[pl.ds(slot * MEMBERS, MEMBERS), :] = full.astype(BF16)


def mid_kernel(before, after, edge, inner, lhs_ref, mean_ref, out_ref, matrices):
    for r in range(PLAT):
        place_packed(matrices, r * WIDE, before, r)
        place_packed(matrices, r * WIDE + PLON + 1, after, r)
        for c in range(PLON):
            p = r * PLON + c
            value = edge[EDGE.index(p)] if p in EDGE else inner[INNER.index(p)]
            matrices[pl.ds((r * WIDE + c + 1) * MEMBERS, MEMBERS), :] = value

    out_ref[...] = dot_nn(lhs_ref[...], matrices[...]) + mean_ref[:, 0:1]


def rim_kernel(above_edge, below_edge, above, below, lhs_ref, base_ref, out_ref, matrices):
    for row, edge, rest in ((0, above_edge, above), (1, below_edge, below)):
        for i, c in enumerate((0, PLON - 1)):
            place_packed(matrices, row * WIDE + c + 1, edge, i)
        for i, c in enumerate([-1] + list(range(1, PLON - 1)) + [PLON]):
            place_packed(matrices, row * WIDE + c + 1, rest, i)

    out_ref[...] = (dot_nn(lhs_ref[...], matrices[...]) + base_ref[...]).astype(BF16)


def mix(kernel, transforms, lhs, base, dtype):
    cells, depth = lhs.shape
    return pl.pallas_call(
        kernel,
        out_shape=jax.ShapeDtypeStruct((cells, MEMBERS), dtype),
        in_specs=[VMEM_SPEC] * (len(transforms) + 2),
        out_specs=VMEM_SPEC,
        scratch_shapes=[pltpu.VMEM((depth, MEMBERS), BF16)],
        compiler_params=params(20),
        cost_estimate=pl.CostEstimate(
            flops=2 * cells * depth * MEMBERS, bytes_accessed=cells * depth * 2, transcendentals=0),
    )(*transforms, lhs, base)


def on_device(obs_pert, obs_weight, innovation, batch_len, batch_owner, batch_points, batch_count,
              batch_taper, background, stencil, frac):
    lon_size, lat_size = lax.axis_size("lon"), lax.axis_size("lat")
    lat_pos, lon_pos = lax.axis_index("lat"), lax.axis_index("lon")
    me = lon_pos.astype(jnp.int32).reshape(1)
    pos = jnp.stack([lat_pos, lon_pos]).astype(jnp.int32)
    fixed = (me, batch_owner.T, batch_len, batch_points.T, batch_count, obs_weight, innovation, batch_taper.T,
             obs_pert)
    half = lon_size // 2

    def swap(value, offset):
        return lax.ppermute(value, "lon", [(i, i ^ offset) for i in range(lon_size)])

    far = batch_blocks(57, half + 1, half - 1, lon_size, *fixed)
    relayed = [swap(far[i - 1], i) for i in range(half - 1, 0, -1)]
    *near, own_far = batch_blocks(57, 1, half, lon_size, *fixed)
    got = [swap(near[i - 1], i) for i in range(half - 1, 0, -1)]
    obs_pert, near, own_far = lax.optimization_barrier((obs_pert, near, own_far))
    own_near, = batch_blocks(57, 0, 1, lon_size, *fixed[:-1], obs_pert)
    relayed, own_near = lax.optimization_barrier((relayed, own_near))
    far_edge, far_inner = relay_sums([own_far] + relayed)
    far_edge, far_inner, background = lax.optimization_barrier((far_edge, far_inner, background))
    mid_lhs, rim_lhs, mean, own_near = cell_parts(PLON * lon_size, pos, stencil, frac, background, own_near)
    got = [own_near] + got
    far_edge = swap(far_edge, half)
    far_inner, mid_lhs, rim_lhs, mean = lax.optimization_barrier((far_inner, mid_lhs, rim_lhs, mean))
    far_inner = swap(far_inner, half)

    total, side = near_sums(got)
    left, right, *edge_rows, edge = edge_transforms(total, side, far_edge)
    up = [(i, (i + 1) % lon_size) for i in range(lon_size)]
    down = [(j, i) for i, j in up]
    north = [(i, i + 1) for i in range(lat_size - 1)]
    south = [(j, i) for i, j in north]
    before = lax.ppermute(right, "lon", up)
    after = lax.ppermute(left, "lon", down)
    above_edge = lax.ppermute(edge_rows[PLAT - 1], "lat", north)
    below_edge = lax.ppermute(edge_rows[0], "lat", south)
    far_inner, above_edge, below_edge = lax.optimization_barrier((far_inner, above_edge, below_edge))
    inner, *rows = inner_transforms(total, side, far_inner)
    rows = [rows[r].at[0].set(before[r]).at[PLON - 1].set(after[r]) for r in range(PLAT)]
    above = lax.ppermute(rows[PLAT - 1], "lat", north)
    below = lax.ppermute(rows[0], "lat", south)
    partial = mix(mid_kernel, [before, after, edge, inner], mid_lhs, mean, F32)
    return mix(rim_kernel, [above_edge, below_edge, above, below], rim_lhs, partial, BF16).reshape(background.shape)


def solution(mesh):
    return jax.shard_map(
        on_device,
        mesh=mesh,
        in_specs=(
            P(("lat", "lon"), None, None),
            P(("lat", "lon"), None),
            P(("lat", "lon"), None),
            P(("lat", "lon"), None),
            P(("lat", "lon"), None),
            P(("lat", "lon"), None),
            P(("lat", "lon")),
            P(("lat", "lon"), None),
            P("lat", "lon", None),
            P(None, "lat", "lon"),
            P(None, "lat", "lon"),
        ),
        out_specs=P("lat", "lon", None),
        check_vma=False,
    )
```

```python
import functools

import jax
import jax.numpy as jnp
from jax import lax
from jax.experimental import pallas as pl
from jax.experimental.pallas import tpu as pltpu
from jax.sharding import PartitionSpec as P

CAP = 4
PLAT = 2
PLON = 4
POINTS = PLAT * PLON
ITERS = 6
HALF = 128
MEMBERS = 2 * HALF
TILE = 16
BLOCK = CAP * MEMBERS + TILE
PACKED = MEMBERS + TILE
F32 = jnp.float32
BF16 = jnp.bfloat16
MIB = 1024 * 1024

SMEM_SPEC = pl.BlockSpec(memory_space=pltpu.SMEM)
VMEM_SPEC = pl.BlockSpec(memory_space=pltpu.VMEM)
ANY_SPEC = pl.BlockSpec(memory_space=pl.ANY)


def params(mebibytes):
    return pltpu.CompilerParams(vmem_limit_bytes=mebibytes * MIB)


def dot_nn(a, b):
    return lax.dot_general(a, b, (((1,), (0,)), ((), ())), preferred_element_type=F32)


def dot_nt(a, b):
    return lax.dot_general(a, b, (((1,), (1,)), ((), ())), preferred_element_type=F32)


def iota(shape, dim):
    return lax.broadcasted_iota(jnp.int32, shape, dim)


def gram_kernel(first, count, lon_size, me_ref, *refs):
    owner_hbm, len_hbm, points_hbm, num_hbm, weight_hbm, innov_hbm, taper_hbm, pert_ref = refs[:8]
    outs = refs[8:8 + count]
    (owner_ref, len_ref, points_ref, num_ref, weight_ref, innov_ref, taper_ref,
     source, filled, rows, w32, i32, t32, built, small_sem, in_sem, out_sem) = refs[8 + count:]
    held, nobs, _ = pert_ref.shape
    me = me_ref[0]
    loads = [
        pltpu.make_async_copy(a, b, small_sem.at[n])
        for n, (a, b) in enumerate((
            (owner_hbm, owner_ref), (len_hbm, len_ref), (points_hbm, points_ref), (num_hbm, num_ref),
            (weight_hbm, weight_ref), (innov_hbm, innov_ref), (taper_hbm, taper_ref)))]
    for load in loads:
        load.start()

    @pl.loop(0, lon_size)
    def _(k):
        filled[k] = 0

    @pl.loop(0, count * CAP)
    def _(s):
        source[first * CAP + s] = 0

    loads[0].wait()

    @pl.loop(0, held)
    def _(b):
        k = owner_ref[0, b] ^ me
        n = filled[k]
        source[k * CAP + n] = b
        filled[k] = n + 1

    def fetch(step, j):
        b = source[(first + step) * CAP + j]
        return pltpu.make_async_copy(pert_ref.at[b], rows.at[step, j], in_sem.at[step, j])

    @pl.loop(0, count)
    def _(step):
        for j in range(CAP):
            fetch(step, j).start()

    for load in loads[1:]:
        load.wait()
    w32[...] = weight_ref[...].astype(F32)
    i32[...] = innov_ref[...].astype(F32)
    t32[...] = jnp.concatenate(
        [taper_ref[...].astype(F32), jnp.zeros((8 - taper_ref.shape[0], held), F32)], axis=0)
    lane_obs = iota((1, nobs), 1)
    lane = iota((1, HALF), 1)
    lane_held = iota((1, held), 1)
    row_id = iota((HALF, HALF), 0)
    col_id = iota((HALF, HALF), 1)

    @pl.loop(0, count)
    def _(step):
        k = first + step
        for j in range(CAP):
            fetch(step, j).wait()
        lo, hi, dg, cf = [], [], [], []
        for j in range(CAP):
            b = source[k * CAP + j]
            present = j < filled[k]
            live = jnp.where(present, len_ref[0, b], 0)
            keep = jnp.where(lane_obs < live, w32[pl.ds(b, 1), :], 0.0)
            pulled = (keep * i32[pl.ds(b, 1), :]).astype(BF16)
            x = rows[step, j]
            scaled = x.T * keep.astype(BF16)
            lhs = jnp.concatenate([scaled, jnp.broadcast_to(pulled, (TILE, nobs))], axis=0)
            gram = dot_nn(lhs, x)
            a11 = gram[0:HALF, 0:HALF]
            a22 = gram[HALF:MEMBERS, HALF:MEMBERS]
            built[step, pl.ds(j * MEMBERS, HALF), :] = jnp.where(row_id <= col_id, a11, a22).astype(BF16)
            built[step, pl.ds(j * MEMBERS + HALF, HALF), :] = gram[0:HALF, HALF:MEMBERS].astype(BF16)
            lo.append(gram[MEMBERS:MEMBERS + 1, 0:HALF])
            hi.append(gram[MEMBERS:MEMBERS + 1, HALF:MEMBERS])
            dg.append(jnp.sum(jnp.where(row_id == col_id, a22, 0.0), axis=0, keepdims=True))
            limit = jnp.where(present, num_ref[b], 0)
            coef = jnp.zeros((1, HALF), F32)
            for q in range(3):
                taper = jnp.sum(jnp.where(lane_held == b, t32[q:q + 1, :], 0.0), axis=1, keepdims=True)
                hit = (lane == points_ref[q, b]) & (q < limit)
                coef = coef + jnp.where(hit, taper, 0.0)
            cf.append(coef)
        built[step, pl.ds(CAP * MEMBERS, TILE), :] = jnp.concatenate(lo + hi + dg + cf, axis=0).astype(BF16)
        for i in range(count):
            @pl.when(step == i)
            def _():
                pltpu.make_async_copy(built.at[i], outs[i], out_sem.at[i]).start()

    for i in range(count):
        pltpu.make_async_copy(built.at[i], outs[i], out_sem.at[i]).wait()


def batch_blocks(room, first, count, lon_size, me, owner, length, points, num, weight, innov, taper, pert):
    held, nobs, members = pert.shape
    return pl.pallas_call(
        functools.partial(gram_kernel, first, count, lon_size),
        out_shape=[jax.ShapeDtypeStruct((BLOCK, HALF), BF16)] * count,
        in_specs=[SMEM_SPEC] + [ANY_SPEC] * 8,
        out_specs=[ANY_SPEC] * count,
        scratch_shapes=[
            pltpu.SMEM(owner.shape, jnp.int32),
            pltpu.SMEM(length.shape, jnp.int32),
            pltpu.SMEM(points.shape, jnp.int32),
            pltpu.SMEM(num.shape, jnp.int32),
            pltpu.VMEM(weight.shape, BF16),
            pltpu.VMEM(innov.shape, BF16),
            pltpu.VMEM(taper.shape, BF16),
            pltpu.SMEM((lon_size * CAP,), jnp.int32),
            pltpu.SMEM((lon_size,), jnp.int32),
            pltpu.VMEM((count, CAP, nobs, members), BF16),
            pltpu.VMEM((held, nobs), F32),
            pltpu.VMEM((held, nobs), F32),
            pltpu.VMEM((8, held), F32),
            pltpu.VMEM((count, BLOCK, HALF), BF16),
            pltpu.SemaphoreType.DMA((7,)),
            pltpu.SemaphoreType.DMA((count, CAP)),
            pltpu.SemaphoreType.DMA((count,)),
        ],
        compiler_params=params(room),
        cost_estimate=pl.CostEstimate(
            flops=count * CAP * 2 * nobs * members * members,
            bytes_accessed=count * CAP * nobs * members * 2, transcendentals=0),
    )(me, owner, length, points, num, weight, innov, taper, pert)


EDGE = [r * PLON + c for r in range(PLAT) for c in (0, PLON - 1)]
INNER = [r * PLON + c for r in range(PLAT) for c in range(1, PLON - 1)]


def unpack(triangle, corner, diagonal):
    row_id = iota((HALF, HALF), 0)
    col_id = iota((HALF, HALF), 1)
    flipped = triangle.T
    a11 = jnp.where(row_id <= col_id, triangle, flipped)
    a22 = jnp.where(row_id > col_id, triangle, jnp.where(row_id == col_id, diagonal, flipped))
    return jnp.concatenate(
        [jnp.concatenate([a11, corner], axis=1), jnp.concatenate([corner.T, a22], axis=1)], axis=0)


def pack(matrix):
    row_id = iota((HALF, HALF), 0)
    col_id = iota((HALF, HALF), 1)
    a22 = matrix[HALF:MEMBERS, HALF:MEMBERS]
    triangle = jnp.where(row_id <= col_id, matrix[0:HALF, 0:HALF], a22)
    diagonal = jnp.sum(jnp.where(row_id == col_id, a22, 0.0), axis=0, keepdims=True)
    return triangle, matrix[0:HALF, HALF:MEMBERS], diagonal


def sum_by_point(blocks, acc, side):
    slots = len(blocks) * CAP
    extras = [blk[pl.ds(CAP * MEMBERS, TILE), :].astype(F32) for blk in blocks]
    low, high, diag, coef = [
        jnp.concatenate([e[CAP * q:CAP * (q + 1)] for e in extras], axis=0).astype(BF16) for q in range(4)]
    pick = (iota((POINTS, HALF), 0) == iota((POINTS, HALF), 1)).astype(BF16)
    by_point = dot_nt(pick, coef).astype(BF16)
    for q, part in enumerate((diag, low, high)):
        side[q] = dot_nn(by_point, part)
    spread = (iota((POINTS * TILE, HALF), 0) // TILE == iota((POINTS * TILE, HALF), 1)).astype(BF16)
    tall = dot_nt(spread, coef).astype(BF16)
    wide = (iota((slots, slots * TILE), 1) // TILE == iota((slots, slots * TILE), 0)).astype(BF16)
    mixing = dot_nn(tall, wide)
    shape = (POINTS * TILE, slots * TILE)
    mixing = jnp.where(iota(shape, 0) % TILE == iota(shape, 1) % TILE, mixing, 0.0).astype(BF16)
    for g in range(0, MEMBERS // TILE, 2):
        pair = []
        for h in (g, g + 1):
            pair.append(jnp.concatenate(
                [blk[pl.ds(j * MEMBERS + h * TILE, TILE), :] for blk in blocks for j in range(CAP)], axis=0))
        summed = dot_nn(mixing, jnp.concatenate(pair, axis=1))
        for p in range(POINTS):
            for h in (0, 1):
                acc[p, pl.ds((g + h) * TILE, TILE), :] = summed[p * TILE:(p + 1) * TILE, h * HALF:(h + 1) * HALF]


def relay_kernel(count, *refs):
    blocks = refs[:count]
    edge_ref, inner_ref, acc, side = refs[count:]
    sum_by_point(blocks, acc, side)
    for ref, listed in ((edge_ref, EDGE), (inner_ref, INNER)):
        rows = []
        for i, p in enumerate(listed):
            ref[pl.ds(i * MEMBERS, MEMBERS), :] = acc[p].astype(BF16)
            rows += [side[q, pl.ds(p, 1), :] for q in range(3)]
        rows.append(jnp.zeros((TILE - len(rows), HALF), F32))
        ref[pl.ds(len(listed) * MEMBERS, TILE), :] = jnp.concatenate(rows, axis=0).astype(BF16)


def relay_sums(blocks):
    return pl.pallas_call(
        functools.partial(relay_kernel, len(blocks)),
        out_shape=[
            jax.ShapeDtypeStruct((len(EDGE) * MEMBERS + TILE, HALF), BF16),
            jax.ShapeDtypeStruct((len(INNER) * MEMBERS + TILE, HALF), BF16),
        ],
        in_specs=[VMEM_SPEC] * len(blocks),
        out_specs=[VMEM_SPEC] * 2,
        scratch_shapes=[
            pltpu.VMEM((POINTS, MEMBERS, HALF), F32),
            pltpu.VMEM((3, POINTS, HALF), F32),
        ],
        compiler_params=params(6 + len(blocks)),
        cost_estimate=pl.CostEstimate(
            flops=len(blocks) * CAP * POINTS * TILE * MEMBERS * HALF,
            bytes_accessed=len(blocks) * BLOCK * HALF * 4, transcendentals=0),
    )(*blocks)


def transform_points(listed, total_of, side_of, far_ref, scratch, full_ref, packed_out):
    w32, z32, wb, gb, zb = scratch
    eye = (iota((MEMBERS, MEMBERS), 0) == iota((MEMBERS, MEMBERS), 1)).astype(F32)
    scales, shifts = [], []
    points = range(len(listed))
    extra = far_ref[pl.ds(len(listed) * MEMBERS, TILE), :].astype(F32)
    for i in points:
        p = listed[i]
        packed = total_of(p) + far_ref[pl.ds(i * MEMBERS, MEMBERS), :].astype(F32)
        diagonal, low, high = [side_of(p)[q] + extra[3 * i + q:3 * i + q + 1] for q in range(3)]
        shifts.append(jnp.concatenate([low, high], axis=1))
        system = unpack(packed[0:HALF], packed[HALF:MEMBERS], diagonal) + (MEMBERS - 1) * eye
        square = jnp.sum(jnp.sum(system * system, axis=0, keepdims=True), axis=1, keepdims=True)
        inv = lax.rsqrt(square)
        inv = inv * (1.5 - 0.5 * square * inv * inv)
        scales.append(inv)
        iterate = system * inv
        root = 1.5 * eye - 0.5 * iterate
        w32[i] = iterate
        wb[i] = iterate.astype(BF16)
        z32[i] = root
        zb[i] = root.astype(BF16)

    def advance():
        for i in points:
            gb[i] = (0.25 * dot_nn(wb[i], wb[i]) - 1.5 * w32[i]).astype(BF16)
        for i in points:
            value = 2.25 * w32[i] + dot_nn(wb[i], gb[i])
            w32[i] = value
            wb[i] = value.astype(BF16)

    advance()

    for sweep in range(ITERS - 2):
        for i in points:
            value = 1.5 * z32[i] - 0.5 * dot_nn(wb[i], zb[i])
            z32[i] = value
            zb[i] = value.astype(BF16)
        advance()

    for i in points:
        z32[i] = 1.5 * z32[i] - 0.5 * dot_nn(wb[i], zb[i])
    for i in points:
        root = z32[i]
        inner = jnp.sum(root * shifts[i], axis=1, keepdims=True)
        mean_weight = jnp.sum(root * inner, axis=0, keepdims=True) * scales[i]
        result = root * jnp.sqrt((MEMBERS - 1) * scales[i])
        column = jnp.broadcast_to(mean_weight, (HALF, MEMBERS)).T
        full_ref[i] = (result + jnp.concatenate([column, column], axis=1)).astype(BF16)
        triangle, corner, diagonal = pack(result)
        extra = jnp.concatenate(
            [diagonal, mean_weight[:, 0:HALF], mean_weight[:, HALF:MEMBERS], jnp.zeros((TILE - 3, HALF), F32)],
            axis=0)
        for ref, where in packed_out(listed[i]):
            ref[where, pl.ds(0, HALF), :] = triangle.astype(BF16)
            ref[where, pl.ds(HALF, HALF), :] = corner.astype(BF16)
            ref[where, pl.ds(MEMBERS, TILE), :] = extra.astype(BF16)


def sum_kernel(count, *refs):
    total_ref, side_ref = refs[count:]
    sum_by_point(refs[:count], total_ref, side_ref)


def near_sums(blocks):
    count = len(blocks)
    return pl.pallas_call(
        functools.partial(sum_kernel, count),
        out_shape=[
            jax.ShapeDtypeStruct((POINTS, MEMBERS, HALF), F32),
            jax.ShapeDtypeStruct((3, POINTS, HALF), F32),
        ],
        in_specs=[VMEM_SPEC] * count,
        out_specs=[VMEM_SPEC] * 2,
        compiler_params=params(6 + count),
        cost_estimate=pl.CostEstimate(
            flops=count * CAP * POINTS * TILE * MEMBERS * HALF, bytes_accessed=count * BLOCK * HALF * 8, transcendentals=0),
    )(*blocks)


def edge_kernel(total_in, side_in, far_ref, left_ref, right_ref, *refs):
    rows, (full_ref, *scratch) = refs[:PLAT], refs[PLAT:]
    transform_points(
        EDGE,
        lambda p: total_in[p],
        lambda p: [side_in[q, pl.ds(p, 1), :] for q in range(3)],
        far_ref, scratch, full_ref,
        lambda p: [
            (left_ref if p % PLON == 0 else right_ref, p // PLON), (rows[p // PLON], 0 if p % PLON == 0 else 1)])


def inner_kernel(total_in, side_in, far_ref, full_ref, *refs):
    rows, scratch = refs[:PLAT], refs[PLAT:]
    transform_points(
        INNER,
        lambda p: total_in[p],
        lambda p: [side_in[q, pl.ds(p, 1), :] for q in range(3)],
        far_ref, scratch, full_ref,
        lambda p: [(rows[p // PLON], p % PLON)])


def newton_scratch(count):
    shape = (count, MEMBERS, MEMBERS)
    return [pltpu.VMEM(shape, F32)] * 2 + [pltpu.VMEM(shape, BF16)] * 3


def edge_transforms(total, side, far):
    count = len(EDGE)
    columns = jax.ShapeDtypeStruct((PLAT, PACKED, HALF), BF16)
    row = jax.ShapeDtypeStruct((2, PACKED, HALF), BF16)
    return pl.pallas_call(
        edge_kernel,
        out_shape=[columns, columns] + [row] * PLAT + [jax.ShapeDtypeStruct((count, MEMBERS, MEMBERS), BF16)],
        in_specs=[VMEM_SPEC] * 3,
        out_specs=[VMEM_SPEC] * (3 + PLAT),
        scratch_shapes=newton_scratch(count),
        compiler_params=params(12),
        cost_estimate=pl.CostEstimate(
            flops=count * 15 * 2 * MEMBERS ** 3, bytes_accessed=count * MEMBERS * HALF * 6, transcendentals=0),
    )(total, side, far)


def inner_transforms(total, side, far):
    count = len(INNER)
    row = jax.ShapeDtypeStruct((PLON, PACKED, HALF), BF16)
    return pl.pallas_call(
        inner_kernel,
        out_shape=[jax.ShapeDtypeStruct((count, MEMBERS, MEMBERS), BF16)] + [row] * PLAT,
        in_specs=[VMEM_SPEC] * 3,
        out_specs=[VMEM_SPEC] * (1 + PLAT),
        scratch_shapes=newton_scratch(count),
        compiler_params=params(12),
        cost_estimate=pl.CostEstimate(
            flops=count * 15 * 2 * MEMBERS ** 3, bytes_accessed=count * MEMBERS * HALF * 6, transcendentals=0),
    )(total, side, far)


WIDE = PLON + 2
WINDOW = (PLAT + 2) * WIDE


def window_id(row, column):
    return (row + 1) * WIDE + column + 1


ENDS = (0, PLON - 1)
REST = [-1] + list(range(1, PLON - 1)) + [PLON]
OWN = [window_id(r, c) for r in range(PLAT) for c in range(PLON)]
SIDE = [window_id(r, c) for c in (-1, PLON) for r in range(PLAT)] + [
    window_id(r, c) for r in (-1, PLAT) for c in ENDS]
RIM = [window_id(r, c) for r in (-1, PLAT) for c in REST]


def cell_kernel(point_cols, pos_ref, stencil_ref, frac_ref, field_ref, kept_in, own_ref, edge_ref, rim_ref, mean_ref,
                kept_out):
    width = stencil_ref.shape[2]
    lat_pos, lon_pos = pos_ref[0], pos_ref[1]
    i = pl.program_id(0)

    @pl.when(i == 0)
    def _():
        kept_out[...] = kept_in[...]

    ids = iota((HALF, width), 0)
    field = field_ref[0].astype(F32)
    mean = jnp.mean(field, axis=1, keepdims=True)
    mean_ref[...] = jnp.broadcast_to(mean, mean_ref.shape)
    dev = (field - mean).astype(BF16).astype(F32)
    row_off = stencil_ref[0, pl.ds(i, 1), :] - (lat_pos * PLAT - 1)
    col_off = stencil_ref[1, pl.ds(i, 1), :] - (lon_pos * PLON - 1)
    col_off = jnp.where(col_off < 0, col_off + point_cols, col_off)
    col_off = jnp.where(col_off >= point_cols, col_off - point_cols, col_off)
    y = frac_ref[0, pl.ds(i, 1), :]
    x = frac_ref[1, pl.ds(i, 1), :]
    corner = row_off * WIDE + col_off
    weights = jnp.where(corner == ids, (1.0 - y) * (1.0 - x), 0.0)
    weights = weights + jnp.where(corner + WIDE == ids, y * (1.0 - x), 0.0)
    weights = weights + jnp.where(corner + 1 == ids, (1.0 - y) * x, 0.0)
    weights = weights + jnp.where(corner + WIDE + 1 == ids, y * x, 0.0)
    turned = weights.T
    for ref, listed in ((own_ref, OWN), (edge_ref, SIDE), (rim_ref, RIM)):
        for n, point in enumerate(listed):
            ref[:, n * MEMBERS:(n + 1) * MEMBERS] = (dev * turned[:, point:point + 1]).astype(BF16)


def cell_parts(point_cols, pos, stencil, frac, background, kept):
    rows, width, members = background.shape
    cells = rows * width
    return pl.pallas_call(
        functools.partial(cell_kernel, point_cols),
        grid=(rows,),
        out_shape=[
            jax.ShapeDtypeStruct((cells, len(OWN) * members), BF16),
            jax.ShapeDtypeStruct((cells, len(SIDE) * members), BF16),
            jax.ShapeDtypeStruct((cells, len(RIM) * members), BF16),
            jax.ShapeDtypeStruct((cells, HALF), F32),
            jax.ShapeDtypeStruct(kept.shape, kept.dtype),
        ],
        in_specs=[
            SMEM_SPEC,
            pl.BlockSpec(stencil.shape, lambda i: (0, 0, 0)),
            pl.BlockSpec(frac.shape, lambda i: (0, 0, 0)),
            pl.BlockSpec((1, width, members), lambda i: (i, 0, 0)),
            pl.BlockSpec(kept.shape, lambda i: (0, 0)),
        ],
        out_specs=[
            pl.BlockSpec((width, len(OWN) * members), lambda i: (i, 0)),
            pl.BlockSpec((width, len(SIDE) * members), lambda i: (i, 0)),
            pl.BlockSpec((width, len(RIM) * members), lambda i: (i, 0)),
            pl.BlockSpec((width, HALF), lambda i: (i, 0)),
            pl.BlockSpec(kept.shape, lambda i: (0, 0)),
        ],
        compiler_params=params(12),
        cost_estimate=pl.CostEstimate(
            flops=cells * members * WINDOW, bytes_accessed=cells * members * (2 * WINDOW + 4), transcendentals=0),
    )(pos, stencil, frac, background, kept)


def place_packed(matrices, slot, ref, i):
    extra = ref[i, pl.ds(MEMBERS, TILE), :].astype(F32)
    full = unpack(ref[i, pl.ds(0, HALF), :].astype(F32), ref[i, pl.ds(HALF, HALF), :].astype(F32), extra[0:1])
    row = jnp.concatenate([extra[1:2], extra[2:3]], axis=1)
    column = jnp.broadcast_to(row, (HALF, MEMBERS)).T
    full = full + jnp.concatenate([column, column], axis=1)
    matrices[pl.ds(slot * MEMBERS, MEMBERS), :] = full.astype(BF16)


def own_kernel(edge, inner, lhs_ref, mean_ref, out_ref, matrices):
    for p in range(POINTS):
        value = edge[EDGE.index(p)] if p in EDGE else inner[INNER.index(p)]
        matrices[pl.ds(p * MEMBERS, MEMBERS), :] = value
    out_ref[...] = dot_nn(lhs_ref[...], matrices[...]) + mean_ref[:, 0:1]


def side_kernel(before, after, above_edge, below_edge, lhs_ref, base_ref, out_ref, matrices):
    for n, ref in enumerate((before, after, above_edge, below_edge)):
        for i in range(2):
            place_packed(matrices, 2 * n + i, ref, i)
    out_ref[...] = dot_nn(lhs_ref[...], matrices[...]) + base_ref[...]


def rim_kernel(above, below, lhs_ref, base_ref, out_ref, matrices):
    for n, ref in enumerate((above, below)):
        for i in range(PLON):
            place_packed(matrices, n * PLON + i, ref, i)
    out_ref[...] = (dot_nn(lhs_ref[...], matrices[...]) + base_ref[...]).astype(BF16)


def mix(kernel, transforms, lhs, base, dtype):
    cells, depth = lhs.shape
    return pl.pallas_call(
        kernel,
        out_shape=jax.ShapeDtypeStruct((cells, MEMBERS), dtype),
        in_specs=[VMEM_SPEC] * (len(transforms) + 2),
        out_specs=VMEM_SPEC,
        scratch_shapes=[pltpu.VMEM((depth, MEMBERS), BF16)],
        compiler_params=params(20),
        cost_estimate=pl.CostEstimate(
            flops=2 * cells * depth * MEMBERS, bytes_accessed=cells * depth * 2, transcendentals=0),
    )(*transforms, lhs, base)


def on_device(obs_pert, obs_weight, innovation, batch_len, batch_owner, batch_points, batch_count,
              batch_taper, background, stencil, frac):
    lon_size, lat_size = lax.axis_size("lon"), lax.axis_size("lat")
    lat_pos, lon_pos = lax.axis_index("lat"), lax.axis_index("lon")
    me = lon_pos.astype(jnp.int32).reshape(1)
    pos = jnp.stack([lat_pos, lon_pos]).astype(jnp.int32)
    fixed = (me, batch_owner.T, batch_len, batch_points.T, batch_count, obs_weight, innovation, batch_taper.T,
             obs_pert)
    half = lon_size // 2

    def swap(value, offset):
        return lax.ppermute(value, "lon", [(i, i ^ offset) for i in range(lon_size)])

    far = batch_blocks(57, half + 1, half - 1, lon_size, *fixed)
    relayed = [swap(far[i - 1], i) for i in range(half - 1, 0, -1)]
    *near, own_far = batch_blocks(57, 1, half, lon_size, *fixed)
    got = [swap(near[i - 1], i) for i in range(half - 1, 0, -1)]
    obs_pert, near, own_far = lax.optimization_barrier((obs_pert, near, own_far))
    own_near, = batch_blocks(57, 0, 1, lon_size, *fixed[:-1], obs_pert)
    relayed, own_near = lax.optimization_barrier((relayed, own_near))
    far_edge, far_inner = relay_sums([own_far] + relayed)
    far_edge, far_inner, background = lax.optimization_barrier((far_edge, far_inner, background))
    own_lhs, side_lhs, rim_lhs, mean, own_near = cell_parts(PLON * lon_size, pos, stencil, frac, background, own_near)
    got = [own_near] + got
    far_edge = swap(far_edge, half)
    far_inner, own_lhs, side_lhs, rim_lhs, mean = lax.optimization_barrier((far_inner, own_lhs, side_lhs, rim_lhs, mean))
    far_inner = swap(far_inner, half)

    total, side = near_sums(got)
    left, right, *edge_rows, edge = edge_transforms(total, side, far_edge)
    up = [(i, (i + 1) % lon_size) for i in range(lon_size)]
    down = [(j, i) for i, j in up]
    north = [(i, i + 1) for i in range(lat_size - 1)]
    south = [(j, i) for i, j in north]
    before = lax.ppermute(right, "lon", up)
    after = lax.ppermute(left, "lon", down)
    above_edge = lax.ppermute(edge_rows[PLAT - 1], "lat", north)
    below_edge = lax.ppermute(edge_rows[0], "lat", south)
    far_inner, above_edge, below_edge = lax.optimization_barrier((far_inner, above_edge, below_edge))
    inner, *rows = inner_transforms(total, side, far_inner)
    partial = mix(own_kernel, [edge, inner], own_lhs, mean, F32)
    rows, partial = lax.optimization_barrier((rows, partial))
    rows = [rows[r].at[0].set(before[r]).at[PLON - 1].set(after[r]) for r in range(PLAT)]
    above = lax.ppermute(rows[PLAT - 1], "lat", north)
    below = lax.ppermute(rows[0], "lat", south)
    partial = mix(side_kernel, [before, after, above_edge, below_edge], side_lhs, partial, F32)
    return mix(rim_kernel, [above, below], rim_lhs, partial, BF16).reshape(background.shape)


def solution(mesh):
    return jax.shard_map(
        on_device,
        mesh=mesh,
        in_specs=(
            P(("lat", "lon"), None, None),
            P(("lat", "lon"), None),
            P(("lat", "lon"), None),
            P(("lat", "lon"), None),
            P(("lat", "lon"), None),
            P(("lat", "lon"), None),
            P(("lat", "lon")),
            P(("lat", "lon"), None),
            P("lat", "lon", None),
            P(None, "lat", "lon"),
            P(None, "lat", "lon"),
        ),
        out_specs=P("lat", "lon", None),
        check_vma=False,
    )
```
